32 devices in a mesh: groups: 2 (over y), seq: 4 (over z), head: 2 (over x), sub: 2 (over core).
Axes of the slice: x: 2, y: 2, z: 4, core: 2. Of those that a mesh axis runs over, the one named last changes fastest.
Arguments:
- tokens: int32 [3, 4096], P(None, ('groups', 'seq')), parts along dimension 1, may hold values from 0 to 1023
- masked: int32 [4096], P(('groups', 'seq')), parts along dimension 0, may hold values 0 or 1
- used_frames: int32 [2], P('groups'), parts along dimension 0, may hold values from 1024 to 2048
- tables: bfloat16 [3, 1024, 1024], P(None, None, ('head', 'sub')), may hold values from -6 to 6
- mask_vec: bfloat16 [1024], P(('head', 'sub')), may hold values from -6 to 6
- attn_in: bfloat16 [3, 1024, 512], P(None, None, ('head', 'sub')), may hold values from -0.1875 to 0.1875
- head_temp: float32 [8], P(('head', 'sub')), may hold values from 12 to 28
- attn_out: bfloat16 [512, 1024], P(('head', 'sub')), may hold values from -0.25 to 0.25
- conv_in: bfloat16 [2, 1024, 1024], P(None, None, ('head', 'sub')), may hold values from -0.1875 to 0.1875
- conv_kernel: float32 [31, 1024], P(None, ('head', 'sub')), may hold values from -1 to 1
- conv_out: bfloat16 [1024, 1024], P(('head', 'sub')), may hold values from -0.1875 to 0.1875
- voc_in: bfloat16 [1024, 512], P(('head', 'sub')), may hold values from -0.1875 to 0.1875
- voc_kernel: float32 [7, 512], replicated, may hold values from -2 to 2
- voc_up: bfloat16 [512, 1536], P(('head', 'sub')), may hold values from -0.25 to 0.25
- voc_down: bfloat16 [1536, 512], P(('head', 'sub')), may hold values from -0.15625 to 0.15625
- voc_head: bfloat16 [512, 1282], P(('head', 'sub')), may hold values from -0.25 to 0.25
- head_bias: float32 [1282], replicated, may hold values from 0.5 to 2.5
Outputs:
- features: bfloat16 [4096, 1024], P(('groups', 'seq', 'head', 'sub')), parts along dimension 0
- waveform: float32 [1310720], P(('groups', 'seq', 'head', 'sub')), parts along dimension 0
The draws below stay inside these ranges and needn't reach their ends.
There are 2 independent parts, one for each index of `groups`. The reference program is written for one: setup_inputs(seed, part) draws one part's arguments, and reference() takes and returns one part's arrays. A program takes and returns all parts, laid end to end along the dimension named above; an argument that names none is the same for every part. Nothing has to cross between parts.
All inputs are finite; a program needn't handle non-finite values. No bound on the sum of `masked` on one device may be relied on, other than what follows from the above.
Results may differ from the reference program's by a relative error of at most 0.02.
Values may be sent and summed in bfloat16 or wider, within the bound.
No kernel may reach another device: no remote copies, remote signals or barrier semaphores. Data moves between devices by JAX's collectives and lax.ppermute only.
A program may use at most 64 MiB of HBM per device.

```python
import math
import jax
import jax.numpy as jnp
import numpy as np
from jax import lax

D = 1024
H = 8
CODES = 1024
KW = 31
VW = 512
VF = 1536
VK = 7
NFFT = 1280
HOP = 320
HW = 512
BINS = 641
L = 2048
N_SEQ = 4
N_HEAD = 2
N_SUB = 2


def set_ends(values, key, smallest, top_value):
    extent = values.shape
    spot = [jax.random.randint(jax.random.fold_in(key, axis), (), 0, extent[axis]) for axis in range(len(extent))]
    values = values.at[tuple(spot)].set(smallest)
    longest = extent.index(max(extent))
    spot[longest] = (spot[longest] + 1) % extent[longest]
    return values.at[tuple(spot)].set(top_value)


def levels(own_key, shape, shards, smallest, high):
    level = 1.0
    for axis_at, shards_of in shards:
        draws = jax.random.uniform(jax.random.fold_in(jax.random.fold_in(own_key, 6), axis_at), (shards_of,), jnp.float32, smallest / len(shards), high / len(shards))
        level = level * jnp.repeat(jnp.exp(draws), shape[axis_at] // shards_of).reshape((-1,) + (1,) * (len(shape) - 1 - axis_at))
    return level


def cumulative_ranks(amount, lean):
    loads = [(1 << 20) // math.isqrt(rank ** lean) + 1 for rank in range(1, amount + 1)]
    spread = 1 + sum(loads) // (1 << 30)
    return np.cumsum(np.array([max(1, weight // spread) for weight in loads]))


def ranked(rng, dims, number_of, skew):
    table = cumulative_ranks(number_of, skew)
    lot = jax.random.randint(jax.random.fold_in(rng, 1), dims, 0, int(table[number_of - 1]))
    rank = jnp.searchsorted(jnp.asarray(table, jnp.int32), lot, side="right")
    return jax.random.permutation(jax.random.fold_in(rng, 2), number_of)[rank].astype(jnp.int32)


def centred(own_key, shape, scale, most, split=(), kind=jnp.bfloat16):
    array = jax.random.normal(own_key, shape, jnp.float32) * scale
    if len(split) > 0:
        array = levels(own_key, shape, split, -0.22, 0.18) * array
    return jnp.clip(array, min=-most, max=most).astype(kind)


def setup_inputs(seed: int = 0, part: int = 0) -> dict:
    keys = jax.random.split(jax.random.key(seed), 18)
    part_splits = jax.random.split(jax.random.fold_in(keys[17], part), 18)
    return {
        "tokens": set_ends(ranked(part_splits[0], (3, L), CODES, 2), jax.random.fold_in(part_splits[0], 3), 0, CODES - 1).astype(jnp.int32),
        "masked": set_ends((jax.random.randint(part_splits[1], (L,), 0, 2) < 1).astype(jnp.int32), jax.random.fold_in(part_splits[1], 1), 0, 1),
        "used_frames": jax.random.randint(part_splits[2], (1,), L // 2, L + 1).astype(jnp.int32),
        "tables": centred(keys[3], (3, CODES, D), 1.0, 6.0, ((2, 4),)),
        "mask_vec": centred(keys[4], (D,), 1.0, 6.0, ((0, 4),)),
        "attn_in": centred(keys[5], (3, D, HW), D ** -0.5, 0.1875, ((2, 4),)),
        "head_temp": jnp.clip(jnp.exp(math.log(28.0) - 0.84729786 * jax.random.uniform(keys[6], (H,), jnp.float32) ** levels(keys[6], (H,), ((0, 4),), -0.2, 0.2)), 12.0, 28.0),
        "attn_out": centred(keys[7], (HW, D), HW ** -0.5, 0.25, ((0, 4),)),
        "conv_in": centred(keys[8], (2, D, D), D ** -0.5, 0.1875, ((2, 4),)),
        "conv_kernel": centred(keys[9], (KW, D), KW ** -0.5, 1.0, ((1, 4),), jnp.float32),
        "conv_out": centred(keys[10], (D, D), D ** -0.5, 0.1875, ((0, 4),)),
        "voc_in": centred(keys[11], (D, VW), D ** -0.5, 0.1875, ((0, 4),)),
        "voc_kernel": centred(keys[12], (VK, VW), VK ** -0.5, 2.0, (), jnp.float32),
        "voc_up": centred(keys[13], (VW, VF), VW ** -0.5, 0.25, ((0, 4),)),
        "voc_down": centred(keys[14], (VF, VW), VF ** -0.5, 0.15625, ((0, 4),)),
        "voc_head": centred(keys[15], (VW, 2 * BINS), VW ** -0.5, 0.25, ((0, 4),)),
        "head_bias": jnp.clip(jax.random.uniform(keys[16], (2 * BINS,), jnp.float32, 0.5, 2.5), 0.5, 2.5),
    }


def layer_norm(values):
    average = lax.optimization_barrier(jnp.mean(values, axis=-1, keepdims=True))
    centered = values - average
    return centered * lax.rsqrt(lax.optimization_barrier(jnp.mean(centered * centered, axis=-1, keepdims=True)) + 1e-05)

def unit_heads(projected, head_count):
    row_count = projected.shape[0]
    split_heads = projected.reshape(row_count, head_count, projected.shape[1] // head_count)
    scaled = split_heads * lax.rsqrt(lax.optimization_barrier(jnp.sum(split_heads * split_heads, axis=-1, keepdims=True)) + 1e-06)
    return scaled.astype(jnp.bfloat16)

def depthwise(kernel, rows_in):
    tap_count = kernel.shape[0]
    half_taps = tap_count // 2
    padded_rows = jnp.pad(rows_in.astype(jnp.float32), ((half_taps, half_taps), (0, 0)))
    out_rows = rows_in.shape[0]
    result = jnp.zeros((out_rows, rows_in.shape[1]), jnp.float32)
    for offset in range(tap_count):
        result = result + kernel[offset].astype(jnp.float32) * padded_rows[offset:offset + out_rows]
    return result

def reference(tokens, masked, used_frames, tables, mask_vec, attn_in, head_temp, attn_out, conv_in, conv_kernel, conv_out, voc_in, voc_kernel, voc_up, voc_down, voc_head, head_bias):
    total_frames = tokens.shape[1]
    masked_rows = masked == 1
    level_two = jnp.where(masked_rows[:, None], mask_vec.astype(jnp.float32)[None, :], tables[2][tokens[2]].astype(jnp.float32))
    embedded = (tables[0][tokens[0]].astype(jnp.float32) + tables[1][tokens[1]].astype(jnp.float32) + level_two).astype(jnp.bfloat16)
    normed = layer_norm(embedded.astype(jnp.float32)).astype(jnp.bfloat16)
    head_count = head_temp.shape[0]
    query_normalized = unit_heads(jnp.dot(normed, attn_in[0], preferred_element_type=jnp.float32), head_count)
    key_unit = unit_heads(jnp.dot(normed, attn_in[1], preferred_element_type=jnp.float32), head_count)
    value_rows = jnp.dot(normed, attn_in[2], preferred_element_type=jnp.float32).astype(jnp.bfloat16)
    value_heads = value_rows.reshape(total_frames, head_count, -1)
    lookup_admissible_flags = jnp.arange(total_frames) < used_frames[0]
    block_rows = total_frames // N_SEQ

    def one_head(attender_element):
        asker_vectors_split, lookup_vectors_split, content_vectors_split, similarity_sharpness = attender_element

        def one_block(query_block):
            angular_similarity = jnp.dot(query_block, lookup_vectors_split.T, preferred_element_type=jnp.float32)
            attention_probabilities = jnp.where(lookup_admissible_flags[None, :], jnp.exp(similarity_sharpness * (angular_similarity - 1.0)), 0.0)
            normalizer = lax.optimization_barrier(jnp.sum(attention_probabilities, axis=1, keepdims=True))
            weighted = jnp.dot(attention_probabilities.astype(jnp.bfloat16), content_vectors_split, preferred_element_type=jnp.float32)
            return weighted / normalizer
        blocks_out = lax.map(one_block, asker_vectors_split.reshape(N_SEQ, block_rows, asker_vectors_split.shape[1]))
        return blocks_out.reshape(total_frames, asker_vectors_split.shape[1])
    per_head = lax.map(one_head, (jnp.transpose(query_normalized, (1, 0, 2)), jnp.transpose(key_unit, (1, 0, 2)), jnp.transpose(value_heads, (1, 0, 2)), head_temp))
    attended = jnp.transpose(per_head, (1, 0, 2)).reshape(total_frames, -1).astype(jnp.bfloat16)
    stream = embedded.astype(jnp.float32) + jnp.dot(attended, attn_out, preferred_element_type=jnp.float32)
    conv_normed = layer_norm(stream).astype(jnp.bfloat16)
    gate_value = jnp.dot(conv_normed, conv_in[0], preferred_element_type=jnp.float32)
    gate_signal = jnp.dot(conv_normed, conv_in[1], preferred_element_type=jnp.float32)
    gated_rows = (gate_value * jax.nn.sigmoid(gate_signal)).astype(jnp.bfloat16)
    depth_rows = depthwise(conv_kernel, gated_rows)
    activated = (depth_rows * jax.nn.sigmoid(depth_rows)).astype(jnp.bfloat16)
    group_count = N_HEAD * N_SUB
    channels = activated.shape[1] // group_count
    conv_sum = jnp.zeros(stream.shape, jnp.float32)
    for member in range(group_count):
        group_part = jnp.dot(activated[:, member * channels:(member + 1) * channels], conv_out[member * channels:(member + 1) * channels], preferred_element_type=jnp.float32).astype(jnp.bfloat16)
        conv_sum = conv_sum + lax.optimization_barrier(group_part).astype(jnp.float32)
    features = layer_norm(stream + conv_sum).astype(jnp.bfloat16)
    live_rows = (jnp.arange(total_frames) < used_frames[0])[:, None]
    base_rows = layer_norm(jnp.where(live_rows, jnp.dot(features, voc_in, preferred_element_type=jnp.float32), 0.0))
    vdepth = depthwise(voc_kernel, base_rows)
    inner_rows = layer_norm(vdepth).astype(jnp.bfloat16)
    hidden = jax.nn.gelu(jnp.dot(inner_rows, voc_up, preferred_element_type=jnp.float32), approximate=False).astype(jnp.bfloat16)
    refined = base_rows + jnp.dot(hidden, voc_down, preferred_element_type=jnp.float32)
    head_input = layer_norm(refined).astype(jnp.bfloat16)
    spectrum = jnp.dot(head_input, voc_head, preferred_element_type=jnp.float32) + head_bias
    bin_count = spectrum.shape[1] // 2
    magnitude = jnp.minimum(jnp.exp(spectrum[:, :bin_count]), 100.0)
    phase_rows = spectrum[:, bin_count:]
    real_part = magnitude * jnp.cos(phase_rows)
    imag_part = magnitude * jnp.sin(phase_rows)
    wave_rows = jnp.fft.irfft(lax.complex(real_part, imag_part), n=NFFT, axis=1)
    sample_ids = jnp.arange(NFFT).astype(jnp.float32)
    hann_window = 0.5 - 0.5 * jnp.cos(2.0 * math.pi / NFFT * sample_ids)
    intersection = NFFT // HOP
    framed = (wave_rows * hann_window[None, :]).reshape(total_frames, intersection, HOP)
    envelope = jnp.broadcast_to((hann_window * hann_window).reshape(1, intersection, HOP), framed.shape)
    padded_frames = jnp.pad(framed, ((intersection, intersection), (0, 0), (0, 0)))
    padded_env = jnp.pad(envelope, ((intersection, intersection), (0, 0), (0, 0)))
    audio_sum = jnp.zeros((total_frames, HOP), jnp.float32)
    energy = jnp.zeros((total_frames, HOP), jnp.float32)
    for quarter in range(intersection):
        begin = intersection + intersection // 2 - quarter
        audio_sum = audio_sum + padded_frames[begin:begin + total_frames, quarter]
        energy = energy + padded_env[begin:begin + total_frames, quarter]
    waveform = (audio_sum / energy).reshape(total_frames * HOP)
    return (features, waveform)
```

```python
import math

import jax
import jax.numpy as jnp
import ml_dtypes
import numpy as np
from jax import lax
from jax.experimental import pallas as pl
from jax.experimental.pallas import tpu as pltpu
from jax.sharding import PartitionSpec as P

HOP = 320
LANES = 128
KEY_TILE = 256
EDGE = 32
VMEM_BYTES = 56 * 2**20
F32 = jnp.float32
BF16 = jnp.bfloat16
HBM = pl.BlockSpec(memory_space=pl.ANY)
VMEM = pl.BlockSpec(memory_space=pltpu.VMEM)
SMEM = pl.BlockSpec(memory_space=pltpu.SMEM)


def round_up(value, multiple):
    return -(-value // multiple) * multiple


def row_tile(rows, most):
    return max(t for t in range(16, most + 1, 16) if rows % t == 0)


def shifts():
    heads, subs = lax.axis_size("head"), lax.axis_size("sub")
    return [(dh, ds) for dh in range(heads) for ds in range(subs)]


def member(shift, sign):
    heads, subs = lax.axis_size("head"), lax.axis_size("sub")
    head = lax.rem(lax.axis_index("head") + (sign * shift[0] + heads), heads)
    sub = lax.rem(lax.axis_index("sub") + (sign * shift[1] + subs), subs)
    return head * subs + sub


def rotate(x, axis, by):
    size = lax.axis_size(axis)
    return lax.ppermute(x, axis, [(i, (i + by) % size) for i in range(size)])


def gather_members(x):
    pieces = []
    for dh in range(lax.axis_size("head")):
        base = x if dh == 0 else rotate(x, "head", dh)
        for ds in range(lax.axis_size("sub")):
            pieces.append(base if ds == 0 else rotate(base, "sub", ds))
    return pieces


def send_members(pieces):
    heads, subs = lax.axis_size("head"), lax.axis_size("sub")
    out = []
    for (dh, ds), piece in zip(shifts(), pieces):
        if dh or ds:
            perm = [
                (h * subs + s, (h + dh) % heads * subs + (s + ds) % subs)
                for h in range(heads)
                for s in range(subs)
            ]
            piece = lax.ppermute(piece, ("head", "sub"), perm)
        out.append(piece)
    return out


def ring_block(place):
    size = lax.axis_size("seq")
    place = lax.rem(place + size, size)
    return jnp.where(2 * place < size, 2 * place, 2 * (size - 1 - place) + 1)


def ring_place(block):
    size = lax.axis_size("seq")
    return jnp.where(lax.rem(block, 2) == 0, lax.div(block, 2), size - 1 - lax.div(block, 2))


def ring_send(x, by):
    size = lax.axis_size("seq")
    order = list(range(0, size, 2)) + list(range(1, size, 2))[::-1]
    return lax.ppermute(x, "seq", [(order[i], order[(i + by) % size]) for i in range(size)])


def ring_gather(first, second, stages):
    size = lax.axis_size("seq")
    blocks, sources = [first, second], [(0, 0), (0, 1)]
    ahead, behind = [first, second], [first, second]
    for hop in range(1, size // 2 + 1):
        if 2 * hop == size:
            ahead, behind = [ring_send(ahead[0], 1), None], [None, ring_send(behind[1], -1)]
        else:
            new = [ring_send(ahead[0], 1), ring_send(behind[1], -1)]
            new += [ring_send(ahead[1], 1), ring_send(behind[0], -1)]
            ahead, behind = [new[0], new[2]], [new[3], new[1]]
        done = stages[hop]([p for p in ahead + behind if p is not None])
        ahead = [None if p is None else done.pop(0) for p in ahead]
        behind = [None if p is None else done.pop(0) for p in behind]
        for pieces, way in ((ahead, -1), (behind, 1)):
            for half, piece in enumerate(pieces):
                if piece is not None:
                    blocks.append(piece)
                    sources.append((way * hop, half))
    return blocks, sources


def together(*groups):
    flat = lax.optimization_barrier(tuple(x for g in groups for x in g))
    out, at = [], 0
    for g in groups:
        out.append(list(flat[at : at + len(g)]))
        at += len(g)
    return out


def dot(a, b):
    return jnp.dot(a, b, preferred_element_type=F32)


def normalize(parts, width):
    mean = sum(jnp.sum(p, axis=-1, keepdims=True) for p in parts) * (1.0 / width)
    parts = [p - mean for p in parts]
    var = sum(jnp.sum(p * p, axis=-1, keepdims=True) for p in parts) * (1.0 / width)
    scale = lax.rsqrt(var + 1e-05)
    return [p * scale for p in parts]


def layer_norm(values):
    return normalize([values], values.shape[-1])[0]


def call(kernel, out_shape, in_specs, out_specs, scratch, cost, name):
    return pl.pallas_call(
        kernel,
        out_shape=out_shape,
        in_specs=in_specs,
        out_specs=out_specs,
        scratch_shapes=scratch,
        compiler_params=pltpu.CompilerParams(vmem_limit_bytes=VMEM_BYTES),
        cost_estimate=pl.CostEstimate(flops=0, bytes_accessed=int(cost * 2**20), transcendentals=0),
        name=name,
    )


def embed_kernel(tokens_ref, masked_ref, tables_ref, mask_ref, out_ref):
    rows, codes = out_ref.shape[0], tables_ref.shape[1]
    tile = LANES
    lane = lax.broadcasted_iota(jnp.int32, (tile, LANES), 1)
    mask_row = mask_ref[...].astype(F32)[None, :]

    def column(row):
        return jnp.transpose(jnp.broadcast_to(row, (LANES, tile)))

    for start in range(0, rows, tile):
        masked = column(masked_ref[:, start : start + tile]) == 1
        total = jnp.where(masked[:, :1], mask_row, 0.0)
        for level in range(3):
            ids = column(tokens_ref[level : level + 1, start : start + tile])
            if level == 2:
                ids = jnp.where(masked, -1, ids)
            hot = jnp.concatenate(
                [
                    jnp.where(ids == lane + at, 1.0, 0.0).astype(BF16)
                    for at in range(0, codes, LANES)
                ],
                axis=1,
            )
            total = total + dot(hot, tables_ref[level])
        out_ref[start : start + tile, :] = total.astype(BF16)


def unit_heads(projected, head_size):
    width = projected.shape[1]
    lane = lax.broadcasted_iota(jnp.int32, (1, width), 1)
    squares = projected * projected
    scale = jnp.zeros_like(projected)
    for at in range(0, width, head_size):
        own = (lane >= at) & (lane < at + head_size)
        total = jnp.sum(jnp.where(own, squares, 0.0), axis=-1, keepdims=True)
        scale = jnp.where(own, lax.rsqrt(total + 1e-06), scale)
    return projected * scale


def project_kernel(count, head_size, *refs):
    pieces, (w_ref,) = refs[:count], refs[count : count + 1]
    q_ref, kv_refs, emb_ref, first_ref, last_ref = (
        refs[count + 1],
        refs[count + 2 : count + 4],
        *refs[count + 4 : count + 7],
    )
    w_scr = refs[count + 7]
    rows, piece_cols = pieces[0].shape
    cols = w_ref.shape[2]
    width = q_ref.shape[1]
    model = emb_ref.shape[1]
    owners = [pl.multiple_of(member(s, -1) * piece_cols, piece_cols) for s in shifts()]
    if width != cols:
        w_scr[...] = jnp.zeros_like(w_scr)
    for r in range(count):
        for p in range(3):
            w_scr[r * piece_cols : (r + 1) * piece_cols, p * width : p * width + cols] = w_ref[
                p, pl.ds(owners[r], piece_cols), :
            ]
    half = rows // 2
    tile = row_tile(half, 128)
    for start in range(0, rows, tile):
        at = slice(start, start + tile)
        raw = [piece[at, :] for piece in pieces]
        normed = jnp.concatenate(
            [p.astype(BF16) for p in normalize([p.astype(F32) for p in raw], model)], axis=1
        )
        proj = dot(normed, w_scr[...])
        query = unit_heads(proj[:, :width], head_size).astype(BF16)
        q_ref[at, :] = query
        kv = jnp.concatenate(
            [unit_heads(proj[:, width : 2 * width], head_size), proj[:, 2 * width :]], axis=1
        ).astype(BF16)
        kv_refs[start // half][start % half : start % half + tile, :] = kv
        for r in range(count):
            emb_ref[at, pl.ds(owners[r], piece_cols)] = raw[r]
        for edge_ref, here in (
            (first_ref, slice(0, EDGE) if start == 0 else None),
            (last_ref, slice(tile - EDGE, tile) if start + tile == rows else None),
        ):
            if here is not None:
                for r in range(count):
                    edge_ref[:, pl.ds(owners[r], piece_cols)] = raw[r][here]
                edge_ref[:, model:] = query[here]


def attend_kernel(head_size, sources, seq_size, out_count, slab, *refs):
    used_ref, temp_ref, q_ref = refs[:3]
    kv_refs = refs[3 : 3 + len(sources)]
    out_refs = refs[3 + len(sources) : 3 + len(sources) + out_count]
    kv_scr, acc_scr, att_scr, sems = refs[3 + len(sources) + out_count :]
    me = lax.axis_index("seq")
    used = used_ref[0]
    rows, width = q_ref.shape
    heads = temp_ref.shape[0]
    total = kv_scr.shape[0]
    frame_count = total // seq_size

    place = ring_place(me)

    def transfers(act):
        for at, (ref, (hop, half)) in enumerate(zip(kv_refs, sources)):
            part = ref.shape[0]
            start = pl.multiple_of(ring_block(place + hop) * frame_count + half * part, part)
            copy = pltpu.make_async_copy(ref, kv_scr.at[pl.ds(start, part), :], sems.at[at])
            getattr(copy, act)()

    transfers("start")
    acc_scr[...] = jnp.zeros_like(acc_scr)
    lane = lax.broadcasted_iota(jnp.int32, (1, width), 1)
    own = [(lane >= h * head_size) & (lane < (h + 1) * head_size) for h in range(heads)]
    sharp = [temp_ref[h] * math.log2(math.e) for h in range(heads)]
    transfers("wait")
    tile = row_tile(rows, 128)

    def step(block, carry):
        start = pl.multiple_of(block * KEY_TILE, KEY_TILE)
        key = kv_scr[pl.ds(start, KEY_TILE), :width]
        live = start + lax.broadcasted_iota(jnp.int32, (KEY_TILE, 1), 0) < used
        value = jnp.concatenate(
            [
                jnp.where(live, kv_scr[pl.ds(start, KEY_TILE), width:].astype(F32), 0.0),
                jnp.broadcast_to(jnp.where(live, 1.0, 0.0), (KEY_TILE, width)),
            ],
            axis=1,
        ).astype(BF16)
        for h in range(heads):
            for at in range(0, rows, tile):
                query = q_ref[at : at + tile, :]
                query = jnp.where(own[h], query, jnp.zeros_like(query))
                score = lax.dot_general(
                    query, key, (((1,), (1,)), ((), ())), preferred_element_type=F32
                )
                weight = jnp.exp2(score * sharp[h] - sharp[h]).astype(BF16)
                acc_scr[h, at : at + tile, :] += dot(weight, value)
        return carry

    lax.fori_loop(0, lax.div(used + (KEY_TILE - 1), KEY_TILE), step, 0)
    for at in range(0, rows, tile):
        result = jnp.zeros((tile, width), F32)
        for h in range(heads):
            summed = acc_scr[h, at : at + tile, :]
            result = jnp.where(own[h], summed[:, :width] / summed[:, width:], result)
        att_scr[at : at + tile, :] = result.astype(BF16)
    for shift, out_ref in zip(shifts(), out_refs):
        start = pl.multiple_of(member(shift, 1) * slab, slab)
        out_ref[...] = att_scr[pl.ds(start, out_ref.shape[0]), : out_ref.shape[1]]


def sine_cosine(x):
    turns = jnp.floor(x * (1.0 / math.pi) + 0.5)
    r = x - turns * 3.140625
    r = r - turns * 9.67502593994140625e-4
    r = r - turns * 1.509957990978376432e-7
    sign = 1.0 - 2.0 * (turns - 2.0 * jnp.floor(turns * 0.5))
    z = r * r
    s = -2.5052108385e-08
    for c in (2.7557319224e-06, -1.9841269841e-04, 8.3333333333e-03, -1.6666666667e-01):
        s = s * z + c
    c_ = 2.0876756988e-09
    for c in (-2.7557319224e-07, 2.4801587302e-05, -1.3888888889e-03, 4.1666666667e-02, -0.5):
        c_ = c_ * z + c
    return sign * (r + r * z * s), sign * (1.0 + z * c_)


def pack_kernel(*refs):
    attn_out, conv_in, conv_out, voc_in, voc_up, voc_down, conv_kernel, head = refs[:8]
    own, mine = refs[8:12], refs[12:16]
    k_scr, head_scr, sems = refs[16:]
    group = lax.axis_index("groups") % 2
    taps, split = conv_kernel.shape
    kernel = conv_kernel[...]
    upper = kernel.astype(BF16)
    lower = (kernel - upper.astype(F32)).astype(BF16)
    blank = jnp.zeros((k_scr.shape[0] - taps, split), BF16)
    k_scr[...] = jnp.concatenate(
        [
            jnp.concatenate([upper, blank], axis=0),
            jnp.concatenate([lower, blank], axis=0),
            jnp.zeros((k_scr.shape[0], k_scr.shape[1] - 2 * split), BF16),
        ],
        axis=1,
    )
    bins, rows = head.shape[0] // 2, head.shape[1]
    padded = head_scr.shape[1] // 2
    blank = jnp.zeros((padded - bins, rows), F32)
    values = head[...].astype(F32)
    values = jnp.concatenate([values[:bins], blank, values[bins:], blank], axis=0)
    head_scr[...] = jnp.transpose(values).astype(BF16)
    chunks = (
        (attn_out, conv_out, k_scr),
        (conv_in,),
        (voc_in, voc_down),
        (voc_up, head_scr),
    )
    copies = []
    for at, chunk in enumerate(chunks):
        for side in range(2):
            half = lax.rem(group + side, 2)
            start = 0
            for src in chunk:
                if len(src.shape) == 3:
                    src, part = src.at[half], src.shape[1]
                else:
                    part = src.shape[0] // 2
                    src = src.at[pl.ds(pl.multiple_of(half * part, part), part), :]
                for dst in (own[at].at[side], mine[at])[: 2 - side]:
                    copies.append((src, dst.at[pl.ds(start, part), :]))
                start += part
    copies = [pltpu.make_async_copy(a, b, sems.at[i]) for i, (a, b) in enumerate(copies)]
    for copy in copies:
        copy.start()
    for copy in copies:
        copy.wait()


def fetcher(chunks, sems):
    group = lax.axis_index("groups") % 2
    copies = {}

    def fetch(kind, r, chunk, start, part, dst, base):
        copies[kind, r] = []
        for side in range(2):
            pair = chunks[chunk][r]
            src = pair[side] if len(pair) == 2 else pair[0].at[side]
            half = lax.rem(group + side, 2)
            to = pl.ds(pl.multiple_of(base + half * part, part), part)
            copy = pltpu.make_async_copy(
                src.at[pl.ds(start, part), :], dst.at[to, :], sems.at[len(copies) * 2 - 1 - side]
            )
            copy.start()
            copies[kind, r].append(copy)

    def ready(kind, r):
        for copy in copies[kind, r]:
            copy.wait()

    return fetch, ready


def weight_pairs(refs, chunk_count):
    chunks, at = [], 0
    for _ in range(chunk_count):
        pairs = []
        for dh in range(lax.axis_size("head")):
            for ds in range(lax.axis_size("sub")):
                taken = 1 if dh == 0 else 2
                pairs.append(refs[at : at + taken])
                at += taken
        chunks.append(pairs)
    return chunks, refs[at:]


def first_frame(slab):
    count = lax.axis_size("head") * lax.axis_size("sub")
    return (lax.axis_index("seq") * count + member((0, 0), 1)) * slab


def conv_kernel_body(geo, *refs):
    count, halo, rim, taps = geo
    emb_ref = refs[0]
    att_refs = refs[1 : 1 + count]
    chunks, refs = weight_pairs(refs[1 + count :], 2)
    feat_ref, window_ref, emb_scr, w_out, w_conv, k_conv, w_mix, stream_scr, gate_scr, sems = refs
    win, model = emb_scr.shape
    slab = feat_ref.shape[0]
    first = first_frame(slab)
    total_frames = lax.axis_size("seq") * count * slab
    emb_copy = pltpu.make_async_copy(
        emb_ref.at[pl.ds(pl.multiple_of(member((0, 0), 1) * slab, slab), win), :],
        emb_scr,
        sems.at[8 * count],
    )
    emb_copy.start()
    fetch, ready = fetcher(chunks, sems)
    out_half = w_out.shape[0] // count // 2
    mix_half = w_mix.shape[1] // 2
    tap_half = k_conv.shape[1] // 2
    deep = w_conv.shape[1] // 2
    for r in range(count):
        fetch("out", r, 0, 0, out_half, w_out, r * 2 * out_half)
    for r in range(count):
        fetch("conv", r, 1, 0, deep, w_conv.at[r], 0)
        fetch("taps", r, 0, out_half + mix_half, tap_half, k_conv.at[r], 0)
        fetch("mix", r, 0, out_half, mix_half, w_mix.at[r], 0)

    attended = jnp.concatenate([ref[...] for ref in att_refs], axis=1)
    emb_copy.wait()
    for r in range(count):
        ready("out", r)
    frames = first - halo + lax.broadcasted_iota(jnp.int32, (win, 1), 0)
    inside = (frames >= 0) & (frames < total_frames)
    stream = jnp.where(inside, emb_scr[...].astype(F32) + dot(attended, w_out[...]), 0.0)
    stream_scr[...] = stream
    conv_normed = layer_norm(stream).astype(BF16)

    mid = slab + 2 * rim
    group_cols = w_conv.shape[2]
    lead = halo - rim - taps // 2
    conv_sum = jnp.zeros((mid, model), F32)
    for r in range(count):
        ready("conv", r)
        signal = dot(conv_normed, w_conv[r, deep:, :])
        gated = dot(conv_normed, w_conv[r, :deep, :]) * jax.nn.sigmoid(signal)
        gated = gated.astype(BF16).astype(F32)
        ready("taps", r)
        kernel = k_conv[r, :, : 2 * group_cols].astype(F32)
        kernel = kernel[:, :group_cols] + kernel[:, group_cols:]
        active = []
        for c in range(group_cols // LANES):
            lanes = slice(c * LANES, (c + 1) * LANES)
            gate_scr[c] = gated[:, lanes]
            depth = jnp.zeros((mid, LANES), F32)
            for k in range(taps):
                depth = depth + kernel[k : k + 1, lanes] * gate_scr[c, lead + k : lead + k + mid, :]
            active.append((depth * jax.nn.sigmoid(depth)).astype(BF16))
        ready("mix", r)
        part = dot(jnp.concatenate(active, axis=1), w_mix[r])
        conv_sum = conv_sum + part.astype(BF16).astype(F32)
    features = layer_norm(stream_scr[halo - rim : halo - rim + mid, :] + conv_sum).astype(BF16)
    feat_ref[...] = features[rim : rim + slab]
    window_ref[...] = features


def voc_kernel_body(geo, *refs):
    count, rim, half_voc = geo
    used_ref, window_ref, voc_kernel_ref, bias_ref, table_ref, hann_ref = refs[:6]
    chunks, refs = weight_pairs(refs[6:], 2)
    wave_ref, w_vin, w_up, w_down, w_head, w_table, base_scr, wave_scr, sems = refs
    slab = wave_ref.shape[0]
    first = first_frame(slab)
    total_frames = lax.axis_size("seq") * count * slab
    used = used_ref[0]
    owners = [member(s, -1) for s in shifts()]
    fetch, ready = fetcher(chunks, sems)
    vin_half = w_vin.shape[0] // count // 2
    down_half = w_down.shape[0] // count // 2
    up_half = w_up.shape[0] // count // 2
    head_half = w_head.shape[0] // count // 2
    for r in range(count):
        fetch("vin", r, 0, 0, vin_half, w_vin, owners[r] * 2 * vin_half)
    for r in range(count):
        fetch("up", r, 1, 0, up_half, w_up, owners[r] * 2 * up_half)
    for r in range(count):
        fetch("down", r, 0, vin_half, down_half, w_down, owners[r] * 2 * down_half)
    for r in range(count):
        fetch("head", r, 1, up_half, head_half, w_head, owners[r] * 2 * head_half)
    table_copy = pltpu.make_async_copy(table_ref, w_table, sems.at[8 * count])
    table_copy.start()
    features = window_ref[...]
    mid = features.shape[0]

    for r in range(count):
        ready("vin", r)
    ids = first - rim + lax.broadcasted_iota(jnp.int32, (mid, 1), 0)
    live = (ids >= 0) & (ids < used)
    base = layer_norm(jnp.where(live, dot(features, w_vin[...]), 0.0))
    voc = base.shape[1]
    trim = half_voc + 1
    rows = mid - 2 * trim
    depth = []
    for c in range(voc // LANES):
        lanes = slice(c * LANES, (c + 1) * LANES)
        base_scr[c] = base[:, lanes]
        total = jnp.zeros((rows, LANES), F32)
        for k in range(2 * half_voc + 1):
            total = total + voc_kernel_ref[k : k + 1, lanes] * base_scr[c, 1 + k : 1 + k + rows, :]
        depth.append(total)
    inner = jnp.concatenate(
        [p.astype(BF16) for p in normalize(depth, voc)], axis=1
    )
    for r in range(count):
        ready("up", r)
    up = dot(inner, w_up[...])
    hidden = (0.5 * up * (1.0 + lax.erf(up * math.sqrt(0.5)))).astype(BF16)
    for r in range(count):
        ready("down", r)
    center = jnp.concatenate(
        [base_scr[c, trim : trim + rows, :] for c in range(voc // LANES)], axis=1
    )
    head_input = layer_norm(center + dot(hidden, w_down[...])).astype(BF16)
    for r in range(count):
        ready("head", r)
    spectrum = dot(head_input, w_head[...]) + bias_ref[...]
    bins = spectrum.shape[1] // 2
    magnitude = jnp.minimum(jnp.exp(spectrum[:, :bins]), 100.0)
    sine, cosine = sine_cosine(spectrum[:, bins:])
    coefficients = jnp.concatenate([magnitude * cosine, magnitude * sine], axis=1).astype(BF16)
    table_copy.wait()
    ids = first - rim + trim + lax.broadcasted_iota(jnp.int32, (rows, 1), 0)
    exists = jnp.where((ids >= 0) & (ids < total_frames), 1.0, 0.0)
    parts = wave_scr.shape[0]
    span = wave_scr.shape[2]
    for q in range(parts):
        wave_scr[q] = exists * dot(coefficients, w_table[:, q * span : (q + 1) * span])
    audio = jnp.zeros((slab, span), F32)
    energy = jnp.zeros((slab, span), F32)
    for q in range(parts):
        begin = rim - trim + parts // 2 - q
        audio = audio + wave_scr[q, begin : begin + slab, :]
        energy = energy + exists[begin : begin + slab] * hann_ref[q : q + 1, :]
    wave_ref[...] = audio[:, :HOP] / energy[:, :HOP]


def synthesis(bins, padded, span):
    size = 2 * (bins - 1)
    parts = size // HOP
    k = np.arange(bins)[:, None]
    n = np.arange(size)[None, :]
    angle = 2.0 * np.pi / size * (k * n % size)
    hann = 0.5 - 0.5 * np.cos(2.0 * np.pi / size * np.arange(size))
    edge = (k == 0) | (k == bins - 1)
    factor = np.where(edge, 1.0, 2.0) / size * hann[None, :]
    both = (factor * np.cos(angle), np.where(edge, 0.0, -factor * np.sin(angle)))
    table = np.zeros((2, padded, parts, span), np.float32)
    for at, values in enumerate(both):
        table[at, :bins, :, :HOP] = values.reshape(bins, parts, HOP)
    squares = np.zeros((parts, span), np.float32)
    squares[:, :HOP] = (hann * hann).reshape(parts, HOP)
    return table.reshape(2 * padded, parts * span).astype(ml_dtypes.bfloat16), squares


def local(
    tokens,
    masked,
    used_frames,
    tables,
    mask_vec,
    attn_in,
    head_temp,
    attn_out,
    conv_in,
    conv_kernel,
    conv_out,
    voc_in,
    voc_kernel,
    voc_up,
    voc_down,
    voc_head,
    head_bias,
):
    frame_count = tokens.shape[1]
    count = lax.axis_size("head") * lax.axis_size("sub")
    seq_size = lax.axis_size("seq")
    model = attn_in.shape[1]
    piece_cols = tables.shape[2]
    cols = attn_in.shape[2]
    width = round_up(cols, LANES)
    head_size = cols // head_temp.shape[0]
    slab = frame_count // count
    bins = head_bias.shape[0] // 2
    half_voc = voc_kernel.shape[0] // 2
    parts = 2 * (bins - 1) // HOP
    rim = round_up(half_voc + parts // 2, 8)
    halo = round_up(half_voc + parts // 2 + conv_kernel.shape[0] // 2, 8)
    win = slab + 2 * halo
    mid = slab + 2 * rim
    taps = conv_kernel.shape[0]

    embedded = call(
        embed_kernel,
        jax.ShapeDtypeStruct((frame_count, piece_cols), BF16),
        [VMEM] * 4,
        VMEM,
        [],
        9,
        "embed",
    )(tokens, masked[None, :], tables, mask_vec)
    heads_out = lax.axis_size("head")
    crossed = [rotate(embedded, "head", dh) for dh in range(1, heads_out)]
    beside = rotate(embedded, "sub", 1)
    conv_kernel, embedded = lax.optimization_barrier((conv_kernel, embedded))

    padded = round_up(bins, LANES)
    gap = ((0, 0), (0, padded - bins))
    bias = jnp.pad(head_bias.reshape(2, bins), gap).reshape(1, 2 * padded)
    deep = conv_in.shape[1]
    tap_rows = round_up(taps, 32)
    voc = voc_in.shape[1]
    hidden = voc_up.shape[1]
    shapes = (
        ((attn_out.shape[0] + conv_out.shape[0] + tap_rows) // 2, model),
        (deep, conv_in.shape[2]),
        ((voc_in.shape[0] + voc_down.shape[0]) // 2, voc),
        ((voc_up.shape[0] + voc_head.shape[0]) // 2, hidden),
    )
    packed = call(
        pack_kernel,
        [jax.ShapeDtypeStruct((2,) + shape, BF16) for shape in shapes]
        + [jax.ShapeDtypeStruct(shape, BF16) for shape in shapes],
        [HBM] * 6 + [VMEM] * 2,
        [VMEM] * 8,
        [
            pltpu.VMEM((tap_rows, model), BF16),
            pltpu.VMEM((voc_head.shape[0], 2 * padded), BF16),
            pltpu.SemaphoreType.DMA((24,)),
        ],
        15,
        "pack",
    )(attn_out, conv_in, conv_out, voc_in, voc_up, voc_down, conv_kernel, voc_head.T)
    crossed, packed = together(crossed, packed)
    own, mine = packed[:4], packed[4:]
    pieces = [embedded, beside]
    for piece in crossed:
        pieces += [piece, rotate(piece, "sub", 1)]
    others = range(1, heads_out)
    near, far, near_sub, far_sub, own_sub = [[None] * 4 for _ in range(5)]

    def cross(at):
        near[at] = [rotate(mine[at], "head", dh) for dh in others]

    def spread(at):
        far[at] = [rotate(x, "groups", 1) for x in near[at]]

    def share(at):
        near_sub[at] = [rotate(x, "sub", 1) for x in near[at]]
        far_sub[at] = [rotate(x, "sub", 1) for x in far[at]]

    cross(0)
    cross(1)

    half = frame_count // 2
    q_own, kv_first, kv_second, emb_own, edge_first, edge_last = call(
        lambda *refs: project_kernel(count, head_size, *refs),
        (
            jax.ShapeDtypeStruct((frame_count, width), BF16),
            jax.ShapeDtypeStruct((half, 2 * width), BF16),
            jax.ShapeDtypeStruct((half, 2 * width), BF16),
            jax.ShapeDtypeStruct((frame_count, model), BF16),
            jax.ShapeDtypeStruct((EDGE, model + width), BF16),
            jax.ShapeDtypeStruct((EDGE, model + width), BF16),
        ),
        [VMEM] * (count + 1),
        (VMEM,) * 6,
        [pltpu.VMEM((model, 3 * width), BF16)],
        10,
        "project",
    )(*pieces, attn_in)

    def first_stage(results):
        results, near[0], edges[:], mine[2:], own[:2] = together(
            results, near[0], edges, mine[2:], own[:2]
        )
        spread(0)
        cross(2)
        edges[:] = [rotate(edges[0], "seq", -1), rotate(edges[1], "seq", 1)]
        return results

    def second_stage(results):
        results, near[1], edges[:], mine[3:], own[2:] = together(
            results, near[1], edges, mine[3:], own[2:]
        )
        spread(1)
        cross(3)
        return results

    edges = [edge_first, edge_last]
    stages = {hop: lambda results: results for hop in range(1, seq_size // 2 + 1)}
    stages[1] = first_stage
    stages[max(2, seq_size // 2)] = second_stage
    blocks, sources = ring_gather(kv_first, kv_second, stages)
    after, before = edges[0][:halo], edges[1][EDGE - halo :]
    query = jnp.concatenate([before[:, model:], q_own, after[:, model:]], axis=0)
    emb = jnp.concatenate([before[:, :model], emb_own, after[:, :model]], axis=0)

    rows = frame_count + 2 * halo
    total_frames = seq_size * frame_count
    heads = head_temp.shape[0]
    windows = call(
        lambda *refs: attend_kernel(head_size, sources, seq_size, count, slab, *refs),
        (jax.ShapeDtypeStruct((win, cols), BF16),) * count,
        [SMEM, SMEM, VMEM] + [HBM] * len(blocks),
        (VMEM,) * count,
        [
            pltpu.VMEM((total_frames, 2 * width), BF16),
            pltpu.VMEM((heads, rows, 2 * width), F32),
            pltpu.VMEM((rows, width), BF16),
            pltpu.SemaphoreType.DMA((len(blocks),)),
        ],
        24,
        "attend",
    )(used_frames, head_temp, query, *blocks)
    windows, near[0], far[0], near[2] = together(windows, near[0], far[0], near[2])
    attended = send_members(windows)
    spread(2)
    share(0)
    own_sub[:] = [rotate(x, "sub", 1) for x in own]
    share(1)
    attended, near[3] = together(attended, near[3])
    spread(3)
    share(2)
    share(3)
    weights = []
    for at in range(4):
        weights.append([own[at], own_sub[at]])
        for dh in range(heads_out - 1):
            weights[at] += [near[at][dh], far[at][dh], near_sub[at][dh], far_sub[at][dh]]

    span = round_up(HOP, LANES)
    table, squares = synthesis(bins, padded, span)
    features, window = call(
        lambda *refs: conv_kernel_body((count, halo, rim, taps), *refs),
        (
            jax.ShapeDtypeStruct((slab, model), BF16),
            jax.ShapeDtypeStruct((mid, model), BF16),
        ),
        [HBM] + [VMEM] * count + [HBM] * (len(weights[0]) + len(weights[1])),
        (VMEM, VMEM),
        [
            pltpu.VMEM((win, model), BF16),
            pltpu.VMEM((count * cols, model), BF16),
            pltpu.VMEM((count, 2 * deep, conv_in.shape[2]), BF16),
            pltpu.VMEM((count, tap_rows, model), BF16),
            pltpu.VMEM((count,) + conv_out.shape, BF16),
            pltpu.VMEM((win, model), F32),
            pltpu.VMEM((conv_in.shape[2] // LANES, win, LANES), F32),
            pltpu.SemaphoreType.DMA((8 * count + 1,)),
        ],
        18,
        "conv",
    )(emb, *attended, *weights[0], *weights[1])
    wave = call(
        lambda *refs: voc_kernel_body((count, rim, half_voc), *refs),
        jax.ShapeDtypeStruct((slab, HOP), F32),
        [SMEM] + [VMEM] * 3 + [HBM, VMEM] + [HBM] * (len(weights[2]) + len(weights[3])),
        VMEM,
        [
            pltpu.VMEM((count * voc_in.shape[0], voc), BF16),
            pltpu.VMEM((count * voc_up.shape[0], voc_up.shape[1]), BF16),
            pltpu.VMEM((count * voc_down.shape[0], voc), BF16),
            pltpu.VMEM((count * voc_head.shape[0], 2 * padded), BF16),
            pltpu.VMEM(table.shape, BF16),
            pltpu.VMEM((voc // LANES, mid, LANES), F32),
            pltpu.VMEM((parts, mid - 2 * (half_voc + 1), span), F32),
            pltpu.SemaphoreType.DMA((8 * count + 1,)),
        ],
        18,
        "vocoder",
    )(
        used_frames,
        window,
        voc_kernel,
        bias,
        jnp.asarray(table),
        jnp.asarray(squares),
        *weights[2],
        *weights[3],
    )
    return features, wave.reshape(slab * HOP)


def solution(mesh):
    in_specs = (
        P(None, ("groups", "seq")),
        P(("groups", "seq")),
        P("groups"),
        P(None, None, ("head", "sub")),
        P(("head", "sub")),
        P(None, None, ("head", "sub")),
        P(("head", "sub")),
        P(("head", "sub"), None),
        P(None, None, ("head", "sub")),
        P(None, ("head", "sub")),
        P(("head", "sub"), None),
        P(("head", "sub"), None),
        P(),
        P(("head", "sub"), None),
        P(("head", "sub"), None),
        P(("head", "sub"), None),
        P(),
    )
    out_specs = (P(("groups", "seq", "head", "sub"), None), P(("groups", "seq", "head", "sub")))
    return jax.shard_map(local, mesh=mesh, in_specs=in_specs, out_specs=out_specs, check_vma=False)
```

```python
import math

import jax
import jax.numpy as jnp
import ml_dtypes
import numpy as np
from jax import lax
from jax.experimental import pallas as pl
from jax.experimental.pallas import tpu as pltpu
from jax.sharding import PartitionSpec as P

HOP = 320
LANES = 128
ROWS = 128
COST = 2**36
EDGE = 32
VMEM_BYTES = 56 * 2**20
F32 = jnp.float32
BF16 = jnp.bfloat16
HBM = pl.BlockSpec(memory_space=pl.ANY)
VMEM = pl.BlockSpec(memory_space=pltpu.VMEM)
SMEM = pl.BlockSpec(memory_space=pltpu.SMEM)


def round_up(value, multiple):
    return -(-value // multiple) * multiple


def row_tile(rows, most):
    return max(t for t in range(16, most + 1, 16) if rows % t == 0)


def shifts():
    heads, subs = lax.axis_size("head"), lax.axis_size("sub")
    return [(dh, ds) for dh in range(heads) for ds in range(subs)]


def member(shift, sign):
    heads, subs = lax.axis_size("head"), lax.axis_size("sub")
    head = lax.rem(lax.axis_index("head") + (sign * shift[0] + heads), heads)
    sub = lax.rem(lax.axis_index("sub") + (sign * shift[1] + subs), subs)
    return head * subs + sub


def rotate(x, axis, by):
    size = lax.axis_size(axis)
    return lax.ppermute(x, axis, [(i, (i + by) % size) for i in range(size)])


def send_members(pieces):
    heads, subs = lax.axis_size("head"), lax.axis_size("sub")
    out = []
    for (dh, ds), piece in zip(shifts(), pieces):
        if dh or ds:
            perm = [
                (h * subs + s, (h + dh) % heads * subs + (s + ds) % subs)
                for h in range(heads)
                for s in range(subs)
            ]
            piece = lax.ppermute(piece, ("head", "sub"), perm)
        out.append(piece)
    return out


def together(*groups):
    flat = lax.optimization_barrier(tuple(x for g in groups for x in g))
    out, at = [], 0
    for g in groups:
        out.append(list(flat[at : at + len(g)]))
        at += len(g)
    return out


def dot(a, b):
    return jnp.dot(a, b, preferred_element_type=F32)


def normalize(parts, width):
    mean = sum(jnp.sum(p, axis=-1, keepdims=True) for p in parts) * (1.0 / width)
    parts = [p - mean for p in parts]
    var = sum(jnp.sum(p * p, axis=-1, keepdims=True) for p in parts) * (1.0 / width)
    scale = lax.rsqrt(var + 1e-05)
    return [p * scale for p in parts]


def layer_norm(values):
    return normalize([values], values.shape[-1])[0]


def call(kernel, out_shape, in_specs, out_specs, scratch, cost, name):
    return pl.pallas_call(
        kernel,
        out_shape=out_shape,
        in_specs=in_specs,
        out_specs=out_specs,
        scratch_shapes=scratch,
        compiler_params=pltpu.CompilerParams(vmem_limit_bytes=VMEM_BYTES),
        cost_estimate=pl.CostEstimate(flops=COST, bytes_accessed=0, transcendentals=0),
        name=name,
    )


def embed_kernel(tokens_ref, masked_ref, tables_ref, mask_ref, out_ref):
    rows, codes = out_ref.shape[0], tables_ref.shape[1]
    tile = LANES
    lane = lax.broadcasted_iota(jnp.int32, (tile, LANES), 1)
    mask_row = mask_ref[...].astype(F32)[None, :]

    def column(row):
        return jnp.transpose(jnp.broadcast_to(row, (LANES, tile)))

    for start in range(0, rows, tile):
        masked = column(masked_ref[:, start : start + tile]) == 1
        total = jnp.where(masked[:, :1], mask_row, 0.0)
        for level in range(3):
            ids = column(tokens_ref[level : level + 1, start : start + tile])
            if level == 2:
                ids = jnp.where(masked, -1, ids)
            hot = jnp.concatenate(
                [
                    jnp.where(ids == lane + at, 1.0, 0.0).astype(BF16)
                    for at in range(0, codes, LANES)
                ],
                axis=1,
            )
            total = total + dot(hot, tables_ref[level])
        out_ref[start : start + tile, :] = total.astype(BF16)


def unit_heads(projected, head_size):
    width = projected.shape[1]
    lane = lax.broadcasted_iota(jnp.int32, (1, width), 1)
    squares = projected * projected
    scale = jnp.zeros_like(projected)
    for at in range(0, width, head_size):
        own = (lane >= at) & (lane < at + head_size)
        total = jnp.sum(jnp.where(own, squares, 0.0), axis=-1, keepdims=True)
        scale = jnp.where(own, lax.rsqrt(total + 1e-06), scale)
    return projected * scale


def project_kernel(count, head_size, *refs):
    pieces, w_ref = refs[:count], refs[count]
    rows, piece_cols = pieces[0].shape
    cols = w_ref.shape[2]
    owners = [pl.multiple_of(member(s, -1) * piece_cols, piece_cols) for s in shifts()]
    kinds = (0, 1, 2)
    w_scr = refs[-1]
    width = w_scr.shape[1] // len(kinds)
    if width != cols:
        w_scr[...] = jnp.zeros_like(w_scr)
    for r in range(count):
        for p, kind in enumerate(kinds):
            w_scr[r * piece_cols : (r + 1) * piece_cols, p * width : p * width + cols] = w_ref[
                kind, pl.ds(owners[r], piece_cols), :
            ]
    model = count * piece_cols
    tile = row_tile(rows, 128)
    for start in range(0, rows, tile):
        at = slice(start, start + tile)
        raw = [piece[at, :] for piece in pieces]
        normed = jnp.concatenate(
            [p.astype(BF16) for p in normalize([p.astype(F32) for p in raw], model)], axis=1
        )
        proj = dot(normed, w_scr[...])
        kv = jnp.concatenate(
            [unit_heads(proj[:, -2 * width : -width], head_size), proj[:, -width:]], axis=1
        ).astype(BF16)
        q_ref, emb_ref, up_ref, down_ref = refs[count + 1 : count + 5]
        query = unit_heads(proj[:, :width], head_size).astype(BF16)
        q_ref[at, :] = query
        for r in range(count):
            emb_ref[at, pl.ds(owners[r], piece_cols)] = raw[r]
        for ref in (up_ref, down_ref):
            ref[at, :] = kv
        halo = (up_ref.shape[0] - rows) // (model // (2 * width) + 1)
        for ref, here in (
            (down_ref, slice(0, halo) if start == 0 else None),
            (up_ref, slice(tile - halo, tile) if start + tile == rows else None),
        ):
            if here is not None:
                ref[up_ref.shape[0] - halo :, :] = jnp.concatenate(
                    [query[here], jnp.zeros((halo, width), BF16)], axis=1
                )
                for c in range(model // (2 * width)):
                    lanes = slice(c * 2 * width, (c + 1) * 2 * width)
                    to = rows + c * halo
                    ref[to : to + halo, :] = emb_ref[start + here.start : start + here.stop, lanes]


def value_rows(kv, block, used, width):
    rows = kv.shape[0]
    live = block * rows + lax.broadcasted_iota(jnp.int32, (rows, 1), 0) < used
    return jnp.concatenate(
        [
            jnp.where(live, kv[:, width:].astype(F32), 0.0),
            jnp.broadcast_to(jnp.where(live, 1.0, 0.0), (rows, width)),
        ],
        axis=1,
    ).astype(BF16)


def head_lanes(width, head_size, heads):
    lane = lax.broadcasted_iota(jnp.int32, (1, width), 1)
    return [(lane >= h * head_size) & (lane < (h + 1) * head_size) for h in range(heads)]


def weigh(query, own, sharp, key, value):
    query = jnp.where(own, query, jnp.zeros_like(query))
    score = lax.dot_general(query, key, (((1,), (1,)), ((), ())), preferred_element_type=F32)
    return dot(jnp.exp2(score * sharp - sharp).astype(BF16), value)


def seq_block(hop):
    size = lax.axis_size("seq")
    return lax.rem(lax.axis_index("seq") + (hop + size), size)


def attend_part_kernel(head_size, hops, *refs):
    used_ref, temp_ref, q_ref = refs[:3]
    kv_refs = refs[3 : 3 + len(hops)]
    sums_ref = refs[3 + len(hops)] if len(refs) > 5 + len(hops) else None
    acc_ref, v_scr = refs[-2:]
    rows, width = q_ref.shape
    heads = temp_ref.shape[0]
    own = head_lanes(width, head_size, heads)
    for i, (ref, hop) in enumerate(zip(kv_refs, hops)):
        v_scr[i] = value_rows(ref[:rows, :], seq_block(hop), used_ref[0], width)
    tile = row_tile(rows, ROWS)
    for at in range(0, rows, tile):
        for h in range(heads):
            sharp = temp_ref[h] * math.log2(math.e)
            total = 0.0 if sums_ref is None else sums_ref[h, at : at + tile, :]
            for i, ref in enumerate(kv_refs):
                query = q_ref[at : at + tile, :]
                total = total + weigh(query, own[h], sharp, ref[:rows, :width], v_scr[i])
            acc_ref[h, at : at + tile, :] = total


def attend_last_kernel(head_size, halo, hops, done, out_count, slab, *refs):
    used_ref, temp_ref, q_ref, acc_ref, before_ref, after_ref = refs[:6]
    kv_refs = refs[6 : 6 + len(hops)]
    out_refs = refs[6 + len(hops) : 6 + len(hops) + out_count]
    v_scr, att_scr = refs[6 + len(hops) + out_count :]
    rows, width = q_ref.shape
    heads = temp_ref.shape[0]
    own = head_lanes(width, head_size, heads)
    for i, (ref, hop) in enumerate(zip(kv_refs, hops)):
        v_scr[i] = value_rows(ref[:rows, :], seq_block(hop), used_ref[0], width)
    tile = row_tile(rows, ROWS)
    tiles = [(at, None) for at in range(0, rows, tile)] + [(rows, (before_ref, after_ref))]
    for at, edges in tiles:
        if edges is None:
            query = q_ref[at : at + tile, :]
            blocks = range(done, len(hops))
        else:
            query = jnp.concatenate([r[r.shape[0] - halo :, :width] for r in edges], axis=0)
            blocks = range(len(hops))
        result = jnp.zeros(query.shape, F32)
        for h in range(heads):
            sharp = temp_ref[h] * math.log2(math.e)
            total = acc_ref[h, at : at + tile, :] if edges is None else 0.0
            for i in blocks:
                total = total + weigh(query, own[h], sharp, kv_refs[i][:rows, :width], v_scr[i])
            result = jnp.where(own[h], total[:, :width] / total[:, width:], result)
        result = result.astype(BF16)
        if edges is None:
            att_scr[halo + at : halo + at + tile, :] = result
        else:
            att_scr[:halo, :] = result[:halo]
            att_scr[halo + rows :, :] = result[halo:]
    for shift, out_ref in zip(shifts(), out_refs):
        start = pl.multiple_of(member(shift, 1) * slab, slab)
        out_ref[...] = att_scr[pl.ds(start, out_ref.shape[0]), : out_ref.shape[1]]


def sine_cosine(x):
    turns = jnp.floor(x * (1.0 / math.pi) + 0.5)
    r = x - turns * 3.140625
    r = r - turns * 9.67502593994140625e-4
    r = r - turns * 1.509957990978376432e-7
    sign = 1.0 - 2.0 * (turns - 2.0 * jnp.floor(turns * 0.5))
    z = r * r
    s = -2.5052108385e-08
    for c in (2.7557319224e-06, -1.9841269841e-04, 8.3333333333e-03, -1.6666666667e-01):
        s = s * z + c
    c_ = 2.0876756988e-09
    for c in (-2.7557319224e-07, 2.4801587302e-05, -1.3888888889e-03, 4.1666666667e-02, -0.5):
        c_ = c_ * z + c
    return sign * (r + r * z * s), sign * (1.0 + z * c_)


def pack_kernel(*refs):
    attn_out, conv_in, conv_out, voc_in, voc_up, voc_down, conv_kernel, head = refs[:8]
    own_first, own_rest, mine_first, mine_rest = refs[8:12]
    k_scr, head_scr, sems = refs[12:]
    group = lax.axis_index("groups") % 2
    taps, split = conv_kernel.shape
    kernel = conv_kernel[...]
    upper = kernel.astype(BF16)
    lower = (kernel - upper.astype(F32)).astype(BF16)
    blank = jnp.zeros((k_scr.shape[0] - taps, split), BF16)
    k_scr[...] = jnp.concatenate(
        [
            jnp.concatenate([upper, blank], axis=0),
            jnp.concatenate([lower, blank], axis=0),
            jnp.zeros((k_scr.shape[0], k_scr.shape[1] - 2 * split), BF16),
        ],
        axis=1,
    )
    bins, rows = head.shape[0] // 2, head.shape[1]
    padded = head_scr.shape[1] // 2
    blank = jnp.zeros((padded - bins, rows), F32)
    values = head[...].astype(F32)
    values = jnp.concatenate([values[:bins], blank, values[bins:], blank], axis=0)
    head_scr[...] = jnp.transpose(values).astype(BF16)
    chunks = (
        ((attn_out, conv_out, k_scr), own_first, 0, mine_first),
        ((voc_in, voc_down, voc_up, head_scr), own_rest, 0, mine_rest),
    )
    copies = []
    for sources, own, base, mine in chunks:
        for side in range(2):
            half = lax.rem(group + side, 2)
            start = 0
            for src in sources:
                part = src.shape[0] // 2
                cols = mine.shape[1]
                for c in range(src.shape[1] // cols):
                    piece = src.at[
                        pl.ds(pl.multiple_of(half * part, part), part), pl.ds(c * cols, cols)
                    ]
                    copies.append((piece, own.at[side, pl.ds(base + start, part), :]))
                    if side == 0:
                        copies.append((piece, mine.at[pl.ds(start, part), :]))
                    start += part
    start = own_first.shape[1]
    deep, cols = conv_in.shape[1:]
    part = mine_first.shape[0] - start
    for c in range(mine_first.shape[1] // cols):
        copies.append(
            (
                conv_in.at[group, pl.ds(deep // 2 + c * part, part), :],
                mine_first.at[pl.ds(start, part), pl.ds(c * cols, cols)],
            )
        )
    copies = [pltpu.make_async_copy(a, b, sems.at[i]) for i, (a, b) in enumerate(copies)]
    for copy in copies:
        copy.start()
    for copy in copies:
        copy.wait()


def fetcher(chunks, sems):
    group = lax.axis_index("groups") % 2
    subs = lax.axis_size("sub")
    copies = {}
    used = [0]

    def fetch(
        kind, r, chunk, start, part, dst, base, stride=None, cols=None, lanes=None
    ):
        copies[kind, r] = []
        pieces = chunks[chunk][r]
        here = r < subs
        for side in range(2):
            half = lax.rem(group + side, 2)
            if len(pieces) == 2:
                src = pieces[side]
            else:
                src = pieces[0]
                src = src.at[half if here and stride else side]
            to = pl.ds(pl.multiple_of(base + half * (stride or part), part), part)
            for c in range(dst.shape[1] // cols if cols else 1):
                target = dst.at[to, pl.ds(c * cols, cols)] if cols else dst.at[to, :]
                source = src.at[pl.ds(start + c * part, part), pl.ds(*lanes) if lanes else slice(None)]
                copy = pltpu.make_async_copy(source, target, sems.at[used[0]])
                used[0] += 1
                copy.start()
                copies[kind, r].append(copy)

    def ready(kind, r):
        for copy in copies[kind, r]:
            copy.wait()

    return fetch, ready


def weight_pairs(refs, chunk_count):
    chunks, at = [], 0
    for _ in range(chunk_count):
        pairs = []
        for dh in range(lax.axis_size("head")):
            for ds in range(lax.axis_size("sub")):
                taken = 2 if dh and not ds else 1
                pairs.append(refs[at : at + taken])
                at += taken
        chunks.append(pairs)
    return chunks, refs[at:]


def first_frame(slab):
    count = lax.axis_size("head") * lax.axis_size("sub")
    return (lax.axis_index("seq") * count + member((0, 0), 1)) * slab


def conv_kernel_body(geo, *refs):
    count, halo, rim, taps = geo
    emb_ref, before_ref, after_ref = refs[:3]
    att_refs = refs[3 : 3 + count]
    chunks, refs = weight_pairs(refs[3 + count :], 2)
    feat_ref, window_ref, emb_scr, w_out, w_conv, k_conv, w_mix, stream_scr, gate_scr, sems = refs
    win, model = emb_scr.shape
    slab = feat_ref.shape[0]
    first = first_frame(slab)
    total_frames = lax.axis_size("seq") * count * slab
    me = member((0, 0), 1)
    rows = emb_ref.shape[0]
    own = win - halo
    cols = before_ref.shape[1]
    window = []
    for c in range(model // cols):
        piece, lanes = pl.ds(rows + c * halo, halo), pl.ds(c * cols, cols)
        window += [
            (me == 0, before_ref.at[piece, :], emb_scr.at[pl.ds(0, halo), lanes]),
            (me == count - 1, after_ref.at[piece, :], emb_scr.at[pl.ds(own, halo), lanes]),
        ]
    window += [
        (me == 0, emb_ref.at[pl.ds(0, own), :], emb_scr.at[pl.ds(halo, own), :]),
        (me == count - 1, emb_ref.at[pl.ds(rows - own, own), :], emb_scr.at[pl.ds(0, own), :]),
        (
            (me > 0) & (me < count - 1),
            emb_ref.at[pl.ds(pl.multiple_of(jnp.clip(me * slab - halo, 0, rows - win), halo), win), :],
            emb_scr,
        ),
    ]

    def window_copies(act):
        for at, (here, src, dst) in enumerate(window):
            copy = pltpu.make_async_copy(src, dst, sems.at[18 * count + at])
            pl.when(here)(lambda copy=copy: getattr(copy, act)())

    window_copies("start")
    fetch, ready = fetcher(chunks, sems)
    out_half = w_out.shape[0] // count // 2
    mix_half = w_mix.shape[1] // 2
    tap_half = k_conv.shape[1] // 2
    deep = w_conv.shape[1] // 2
    step = deep // 2
    low_rows = step // (model // w_conv.shape[2])

    def fetch_low(r):
        at = out_half + mix_half + tap_half
        for c in range(step // low_rows):
            lanes = (c * w_conv.shape[2], w_conv.shape[2])
            fetch(
                ("low", c), r, 0, at, low_rows, w_conv.at[r], step + c * low_rows, deep, lanes=lanes
            )

    def ready_low(r):
        if r < lax.axis_size("sub"):
            ready("low", r)
        else:
            for c in range(step // low_rows):
                ready(("low", c), r)

    for r in range(count):
        fetch("out", r, 0, 0, out_half, w_out, r * 2 * out_half)
    for r in range(count):
        fetch("top", r, 1, 0, step, w_conv.at[r], 0, deep)
        if r < lax.axis_size("sub"):
            fetch("low", r, 1, step, step, w_conv.at[r], step, deep)
        else:
            fetch_low(r)
        fetch("taps", r, 0, out_half + mix_half, tap_half, k_conv.at[r], 0)
        fetch("mix", r, 0, out_half, mix_half, w_mix.at[r], 0)

    attended = jnp.concatenate([ref[...] for ref in att_refs], axis=1)
    window_copies("wait")
    for r in range(count):
        ready("out", r)
    frames = first - halo + lax.broadcasted_iota(jnp.int32, (win, 1), 0)
    inside = (frames >= 0) & (frames < total_frames)
    stream = jnp.where(inside, emb_scr[...].astype(F32) + dot(attended, w_out[...]), 0.0)
    stream_scr[...] = stream
    conv_normed = layer_norm(stream).astype(BF16)

    mid = slab + 2 * rim
    group_cols = w_conv.shape[2]
    lead = halo - rim - taps // 2
    conv_sum = jnp.zeros((mid, model), F32)
    for r in range(count):
        ready("top", r)
        ready_low(r)
        signal = dot(conv_normed, w_conv[r, deep:, :])
        gated = dot(conv_normed, w_conv[r, :deep, :]) * jax.nn.sigmoid(signal)
        gated = gated.astype(BF16).astype(F32)
        ready("taps", r)
        kernel = k_conv[r, :, : 2 * group_cols].astype(F32)
        kernel = kernel[:, :group_cols] + kernel[:, group_cols:]
        active = []
        for c in range(group_cols // LANES):
            lanes = slice(c * LANES, (c + 1) * LANES)
            gate_scr[c] = gated[:, lanes]
            depth = jnp.zeros((mid, LANES), F32)
            for k in range(taps):
                depth = depth + kernel[k : k + 1, lanes] * gate_scr[c, lead + k : lead + k + mid, :]
            active.append((depth * jax.nn.sigmoid(depth)).astype(BF16))
        ready("mix", r)
        part = dot(jnp.concatenate(active, axis=1), w_mix[r])
        conv_sum = conv_sum + part.astype(BF16).astype(F32)
    features = layer_norm(stream_scr[halo - rim : halo - rim + mid, :] + conv_sum).astype(BF16)
    feat_ref[...] = features[rim : rim + slab]
    window_ref[...] = features


def voc_kernel_body(geo, *refs):
    count, rim, half_voc = geo
    used_ref, window_ref, voc_kernel_ref, bias_ref, table_ref, hann_ref = refs[:6]
    chunks, refs = weight_pairs(refs[6:], 1)
    wave_ref, w_vin, w_up, w_down, w_head, w_table, base_scr, wave_scr, out_scr, sems = refs
    slab = out_scr.shape[1]
    first = first_frame(slab)
    total_frames = lax.axis_size("seq") * count * slab
    used = used_ref[0]
    owners = [member(s, -1) for s in shifts()]
    fetch, ready = fetcher(chunks, sems)
    vin_half = w_vin.shape[0] // count // 2
    down_half = w_down.shape[0] // count // 2
    up_half = w_up.shape[0] // count // 2
    head_half = w_head.shape[0] // count // 2
    voc = w_vin.shape[1]
    rest = vin_half + down_half
    for r in range(count):
        fetch("vin", r, 0, 0, vin_half, w_vin, owners[r] * 2 * vin_half)
    for r in range(count):
        fetch(
            "up", r, 0, rest, up_half, w_up, owners[r] * 2 * up_half, cols=voc
        )
    for r in range(count):
        fetch("down", r, 0, vin_half, down_half, w_down, owners[r] * 2 * down_half)
    for r in range(count):
        at = up_half * (w_up.shape[1] // voc)
        fetch(
            "head",
            r,
            0,
            rest + at,
            head_half,
            w_head,
            owners[r] * 2 * head_half,
            cols=voc,
        )
    table_copy = pltpu.make_async_copy(table_ref, w_table, sems.at[sems.shape[0] - 1])
    table_copy.start()
    features = window_ref[...]
    mid = features.shape[0]

    for r in range(count):
        ready("vin", r)
    ids = first - rim + lax.broadcasted_iota(jnp.int32, (mid, 1), 0)
    live = (ids >= 0) & (ids < used)
    base = layer_norm(jnp.where(live, dot(features, w_vin[...]), 0.0))
    voc = base.shape[1]
    trim = half_voc + 1
    rows = mid - 2 * trim
    depth = []
    for c in range(voc // LANES):
        lanes = slice(c * LANES, (c + 1) * LANES)
        base_scr[c] = base[:, lanes]
        total = jnp.zeros((rows, LANES), F32)
        for k in range(2 * half_voc + 1):
            total = total + voc_kernel_ref[k : k + 1, lanes] * base_scr[c, 1 + k : 1 + k + rows, :]
        depth.append(total)
    inner = jnp.concatenate(
        [p.astype(BF16) for p in normalize(depth, voc)], axis=1
    )
    for r in range(count):
        ready("up", r)
    up = dot(inner, w_up[...])
    hidden = (0.5 * up * (1.0 + lax.erf(up * math.sqrt(0.5)))).astype(BF16)
    for r in range(count):
        ready("down", r)
    center = jnp.concatenate(
        [base_scr[c, trim : trim + rows, :] for c in range(voc // LANES)], axis=1
    )
    head_input = layer_norm(center + dot(hidden, w_down[...])).astype(BF16)
    for r in range(count):
        ready("head", r)
    spectrum = dot(head_input, w_head[...]) + bias_ref[...]
    bins = spectrum.shape[1] // 2
    magnitude = jnp.minimum(jnp.exp(spectrum[:, :bins]), 100.0)
    sine, cosine = sine_cosine(spectrum[:, bins:])
    coefficients = jnp.concatenate([magnitude * cosine, magnitude * sine], axis=1).astype(BF16)
    table_copy.wait()
    ids = first - rim + trim + lax.broadcasted_iota(jnp.int32, (rows, 1), 0)
    exists = jnp.where((ids >= 0) & (ids < total_frames), 1.0, 0.0)
    parts = wave_scr.shape[0]
    span = wave_scr.shape[2]
    for q in range(parts):
        wave_scr[q] = exists * dot(coefficients, w_table[:, q * span : (q + 1) * span])
    audio = jnp.zeros((slab, span), F32)
    energy = jnp.zeros((slab, span), F32)
    for q in range(parts):
        begin = rim - trim + parts // 2 - q
        audio = audio + wave_scr[q, begin : begin + slab, :]
        energy = energy + exists[begin : begin + slab] * hann_ref[q : q + 1, :]
    audio = audio / energy
    tiles = range(span // LANES)
    for c in tiles:
        out_scr[c] = audio[:, c * LANES : (c + 1) * LANES]
    even, odd = (
        jnp.concatenate([out_scr[c, pl.ds(at, slab // 2, stride=2), :] for c in tiles], axis=1)
        for at in range(2)
    )
    samples = jnp.concatenate([even[:, :HOP], odd[:, :HOP]], axis=1)
    count = 2 * HOP // LANES
    for c in range(count):
        wave_ref[pl.ds(c, slab // 2, stride=count), :] = samples[:, c * LANES : (c + 1) * LANES]


def synthesis(bins, padded, span):
    size = 2 * (bins - 1)
    parts = size // HOP
    k = np.arange(bins)[:, None]
    n = np.arange(size)[None, :]
    angle = 2.0 * np.pi / size * (k * n % size)
    hann = 0.5 - 0.5 * np.cos(2.0 * np.pi / size * np.arange(size))
    edge = (k == 0) | (k == bins - 1)
    factor = np.where(edge, 1.0, 2.0) / size * hann[None, :]
    both = (factor * np.cos(angle), np.where(edge, 0.0, -factor * np.sin(angle)))
    table = np.zeros((2, padded, parts, span), np.float32)
    for at, values in enumerate(both):
        table[at, :bins, :, :HOP] = values.reshape(bins, parts, HOP)
    squares = np.ones((parts, span), np.float32)
    squares[:, :HOP] = (hann * hann).reshape(parts, HOP)
    return table.reshape(2 * padded, parts * span).astype(ml_dtypes.bfloat16), squares


def local(
    tokens,
    masked,
    used_frames,
    tables,
    mask_vec,
    attn_in,
    head_temp,
    attn_out,
    conv_in,
    conv_kernel,
    conv_out,
    voc_in,
    voc_kernel,
    voc_up,
    voc_down,
    voc_head,
    head_bias,
):
    frame_count = tokens.shape[1]
    count = lax.axis_size("head") * lax.axis_size("sub")
    seq_size = lax.axis_size("seq")
    model = attn_in.shape[1]
    piece_cols = tables.shape[2]
    cols = attn_in.shape[2]
    width = round_up(cols, LANES)
    head_size = cols // head_temp.shape[0]
    slab = frame_count // count
    bins = head_bias.shape[0] // 2
    half_voc = voc_kernel.shape[0] // 2
    parts = 2 * (bins - 1) // HOP
    rim = round_up(half_voc + parts // 2, 8)
    halo = round_up(half_voc + parts // 2 + conv_kernel.shape[0] // 2, EDGE)
    win = slab + 2 * halo
    mid = slab + 2 * rim
    taps = conv_kernel.shape[0]

    others = range(1, lax.axis_size("head"))
    group = lax.rem(lax.axis_index("groups"), 2)
    deep = conv_in.shape[1]

    def cross(x):
        return [rotate(x, "head", dh) for dh in others]

    def spread(xs):
        return [rotate(x, "groups", 1) for x in xs]

    def share(xs):
        return [rotate(x, "sub", 1) for x in xs]

    def share_both(kind):
        return share([jnp.stack(pair) for pair in zip(near[kind], far[kind])])

    near, far, both, own, own_sub, mine = {}, {}, {}, {}, {}, {}
    mine["top"] = lax.dynamic_slice(
        conv_in, (group, 0, 0), (1, deep // 2, conv_in.shape[2])
    ).reshape(deep // 2, conv_in.shape[2])
    own["b"] = conv_in
    near["top"] = cross(mine["top"])
    own_sub["b"] = share([own["b"]])

    embedded = call(
        embed_kernel,
        jax.ShapeDtypeStruct((frame_count, piece_cols), BF16),
        [VMEM] * 4,
        VMEM,
        [],
        9,
        "embed",
    )(tokens, masked[None, :], tables, mask_vec)
    crossed = cross(embedded)
    beside = share([embedded])
    [conv_kernel], [embedded], near["top"] = together([conv_kernel], [embedded], near["top"])

    padded = round_up(bins, LANES)
    gap = ((0, 0), (0, padded - bins))
    bias = jnp.pad(head_bias.reshape(2, bins), gap).reshape(1, 2 * padded)
    tap_rows = round_up(taps, 32)
    voc = voc_in.shape[1]
    first_rows = (attn_out.shape[0] + conv_out.shape[0] + tap_rows) // 2
    low_rows = deep // 2 * conv_in.shape[2] // model
    conv_rows = (voc_in.shape[0] + voc_down.shape[0]) // 2
    head_rows = (voc_up.shape[0] * voc_up.shape[1] + voc_head.shape[0] * 2 * padded) // voc // 2
    packed = call(
        pack_kernel,
        [
            jax.ShapeDtypeStruct((2, first_rows, model), BF16),
            jax.ShapeDtypeStruct((2, conv_rows + head_rows, voc), BF16),
            jax.ShapeDtypeStruct((first_rows + low_rows, model), BF16),
            jax.ShapeDtypeStruct((conv_rows + head_rows, voc), BF16),
        ],
        [HBM] * 6 + [VMEM] * 2,
        [VMEM] * 4,
        [
            pltpu.VMEM((tap_rows, model), BF16),
            pltpu.VMEM((voc_head.shape[0], 2 * padded), BF16),
            pltpu.SemaphoreType.DMA((48,)),
        ],
        15,
        "pack",
    )(attn_out, conv_in, conv_out, voc_in, voc_up, voc_down, conv_kernel, voc_head.T)

    crossed, beside, own_sub["b"], packed = together(crossed, beside, own_sub["b"], packed)
    own["a"], own["c"], mine["a"], mine["c"] = packed

    def members(own_piece, beside_piece, others_pieces):
        pieces = [own_piece] + beside_piece
        for piece in others_pieces:
            pieces += [piece] + share([piece])
        return pieces

    pieces = members(embedded, beside, crossed)
    far["top"] = spread(near["top"])
    near["a"] = cross(mine["a"])
    chunk = 2 * width
    message = (frame_count + (model // chunk + 1) * halo, chunk)
    q_own, emb, upward, downward = call(
        lambda *refs: project_kernel(count, head_size, *refs),
        (
            jax.ShapeDtypeStruct((frame_count, width), BF16),
            jax.ShapeDtypeStruct((frame_count, model), BF16),
            jax.ShapeDtypeStruct(message, BF16),
            jax.ShapeDtypeStruct(message, BF16),
        ),
        [VMEM] * (count + 1),
        (VMEM,) * 4,
        [pltpu.VMEM((model, 3 * width), BF16)],
        10,
        "project",
    )(*pieces, attn_in)

    below, above = rotate(upward, "seq", 1), rotate(downward, "seq", -1)
    heads = head_temp.shape[0]

    def attend(hops, blocks, sums):
        return call(
            lambda *refs: attend_part_kernel(head_size, hops, *refs),
            jax.ShapeDtypeStruct((heads, frame_count, chunk), F32),
            [SMEM, SMEM] + [VMEM] * (1 + len(blocks) + len(sums)),
            VMEM,
            [pltpu.VMEM((len(blocks), frame_count, chunk), BF16)],
            10,
            "attend",
        )(used_frames, head_temp, q_own, *blocks, *sums)

    sums = attend([0], [upward], [])
    [below, sums, mine["c"]], near["a"], far["top"] = together(
        [below, sums, mine["c"]], near["a"], far["top"]
    )
    blocks, hops = [upward, below, above], [0, -1, 1]
    ahead, behind = below[:frame_count], above[:frame_count]
    for hop in range(2, seq_size // 2 + 1):
        ahead = rotate(ahead, "seq", 1)
        blocks.append(ahead)
        hops.append(-hop)
        if 2 * hop < seq_size:
            behind = rotate(behind, "seq", -1)
            blocks.append(behind)
            hops.append(hop)
    far["a"], near["c"] = spread(near["a"]), cross(mine["c"])
    sums = attend([-1], [below], [sums])

    sums = attend([1], [above], [sums])
    last, [sums, own["a"], own["c"]], near["top"], far["top"] = together(
        blocks[3:], [sums, own["a"], own["c"]], near["top"], far["top"]
    )
    blocks[3:] = last
    own_sub["a"], own_sub["c"] = share([own["a"]]), share([own["c"]])
    both["top"] = share_both("top")
    windows = call(
        lambda *refs: attend_last_kernel(head_size, halo, hops, 3, count, slab, *refs),
        (jax.ShapeDtypeStruct((win, cols), BF16),) * count,
        [SMEM, SMEM] + [VMEM] * (4 + len(blocks)),
        (VMEM,) * count,
        [
            pltpu.VMEM((len(blocks), frame_count, chunk), BF16),
            pltpu.VMEM((frame_count + 2 * halo, width), BF16),
        ],
        10,
        "attend_last",
    )(used_frames, head_temp, q_own, sums, below, above, *blocks)

    windows, far["a"], near["c"], both["top"], own_sub["a"], own_sub["c"] = together(
        windows, far["a"], near["c"], both["top"], own_sub["a"], own_sub["c"]
    )
    attended = send_members(windows)
    both["a"] = share_both("a")
    far["c"] = spread(near["c"])
    own["top"], own_sub["top"] = own["b"], own_sub["b"]

    def weights(kind):
        found = [own[kind], *own_sub[kind]]
        for dh in range(len(others)):
            found += [t[kind][dh] for t in (near, far, both)]
        return found

    conv_weights = [w for kind in ("a", "top") for w in weights(kind)]
    span = round_up(HOP, LANES)
    table, squares = synthesis(bins, padded, span)
    features, window = call(
        lambda *refs: conv_kernel_body((count, halo, rim, taps), *refs),
        (
            jax.ShapeDtypeStruct((slab, model), BF16),
            jax.ShapeDtypeStruct((mid, model), BF16),
        ),
        [HBM] * 3 + [VMEM] * count + [HBM] * len(conv_weights),
        (VMEM, VMEM),
        [
            pltpu.VMEM((win, model), BF16),
            pltpu.VMEM((count * cols, model), BF16),
            pltpu.VMEM((count, 2 * deep, conv_in.shape[2]), BF16),
            pltpu.VMEM((count, tap_rows, model), BF16),
            pltpu.VMEM((count,) + conv_out.shape, BF16),
            pltpu.VMEM((win, model), F32),
            pltpu.VMEM((conv_in.shape[2] // LANES, win, LANES), F32),
            pltpu.SemaphoreType.DMA((10 * count + 3 + 2 * model // (2 * width) + 8 * count,)),
        ],
        18,
        "conv",
    )(emb, below, above, *attended, *conv_weights)
    [window], far["c"] = together([window], far["c"])
    both["c"] = share_both("c")
    voc_weights = weights("c")
    wave = call(
        lambda *refs: voc_kernel_body((count, rim, half_voc), *refs),
        jax.ShapeDtypeStruct((slab * HOP // LANES, LANES), F32),
        [SMEM] + [VMEM] * 3 + [HBM, VMEM] + [HBM] * len(voc_weights),
        VMEM,
        [
            pltpu.VMEM((count * voc_in.shape[0], voc), BF16),
            pltpu.VMEM((count * voc_up.shape[0], voc_up.shape[1]), BF16),
            pltpu.VMEM((count * voc_down.shape[0], voc), BF16),
            pltpu.VMEM((count * voc_head.shape[0], 2 * padded), BF16),
            pltpu.VMEM(table.shape, BF16),
            pltpu.VMEM((voc // LANES, mid, LANES), F32),
            pltpu.VMEM((parts, mid - 2 * (half_voc + 1), span), F32),
            pltpu.VMEM((span // LANES, slab, LANES), F32),
            pltpu.SemaphoreType.DMA((4 * count + 4 * count * (voc_up.shape[1] // voc) + 1,)),
        ],
        18,
        "vocoder",
    )(
        used_frames,
        window,
        voc_kernel,
        bias,
        jnp.asarray(table),
        jnp.asarray(squares),
        *voc_weights,
    )
    return features, wave.reshape(slab * HOP)


def solution(mesh):
    in_specs = (
        P(None, ("groups", "seq")),
        P(("groups", "seq")),
        P("groups"),
        P(None, None, ("head", "sub")),
        P(("head", "sub")),
        P(None, None, ("head", "sub")),
        P(("head", "sub")),
        P(("head", "sub"), None),
        P(None, None, ("head", "sub")),
        P(None, ("head", "sub")),
        P(("head", "sub"), None),
        P(("head", "sub"), None),
        P(),
        P(("head", "sub"), None),
        P(("head", "sub"), None),
        P(("head", "sub"), None),
        P(),
    )
    out_specs = (P(("groups", "seq", "head", "sub"), None), P(("groups", "seq", "head", "sub")))
    return jax.shard_map(local, mesh=mesh, in_specs=in_specs, out_specs=out_specs, check_vma=False)
```

```python
import math

import jax
import jax.numpy as jnp
import ml_dtypes
import numpy as np
from jax import lax
from jax.experimental import pallas as pl
from jax.experimental.pallas import tpu as pltpu
from jax.sharding import PartitionSpec as P

HOP = 320
LANES = 128
ROWS = 128
COST = 2**36
COSTS = (1, 1, 0, 0)
EDGE = 32
F32 = jnp.float32
BF16 = jnp.bfloat16
HBM = pl.BlockSpec(memory_space=pl.ANY)
VMEM = pl.BlockSpec(memory_space=pltpu.VMEM)
SMEM = pl.BlockSpec(memory_space=pltpu.SMEM)


def round_up(value, multiple):
    return -(-value // multiple) * multiple


def row_tile(rows, most):
    return max(t for t in range(16, most + 1, 16) if rows % t == 0)


def shifts():
    heads, subs = lax.axis_size("head"), lax.axis_size("sub")
    return [(dh, ds) for dh in range(heads) for ds in range(subs)]


def member(shift, sign):
    heads, subs = lax.axis_size("head"), lax.axis_size("sub")
    head = lax.rem(lax.axis_index("head") + (sign * shift[0] + heads), heads)
    sub = lax.rem(lax.axis_index("sub") + (sign * shift[1] + subs), subs)
    return head * subs + sub


def rotate(x, axis, by):
    size = lax.axis_size(axis)
    return lax.ppermute(x, axis, [(i, (i + by) % size) for i in range(size)])


def send_members(pieces):
    heads, subs = lax.axis_size("head"), lax.axis_size("sub")
    out = []
    for (dh, ds), piece in zip(shifts(), pieces):
        if dh or ds:
            perm = [
                (h * subs + s, (h + dh) % heads * subs + (s + ds) % subs)
                for h in range(heads)
                for s in range(subs)
            ]
            piece = lax.ppermute(piece, ("head", "sub"), perm)
        out.append(piece)
    return out


def together(*groups):
    flat = lax.optimization_barrier(tuple(x for g in groups for x in g))
    out, at = [], 0
    for g in groups:
        out.append(list(flat[at : at + len(g)]))
        at += len(g)
    return out


def dot(a, b):
    return jnp.dot(a, b, preferred_element_type=F32)


def normalize(parts, width):
    mean = sum(jnp.sum(p, axis=-1, keepdims=True) for p in parts) * (1.0 / width)
    parts = [p - mean for p in parts]
    var = sum(jnp.sum(p * p, axis=-1, keepdims=True) for p in parts) * (1.0 / width)
    scale = lax.rsqrt(var + 1e-05)
    return [p * scale for p in parts]


def layer_norm(values):
    return normalize([values], values.shape[-1])[0]


def call(kernel, out_shape, in_specs, out_specs, scratch, cost, name):
    return pl.pallas_call(
        kernel,
        out_shape=out_shape,
        in_specs=in_specs,
        out_specs=out_specs,
        scratch_shapes=scratch,
        compiler_params=pltpu.CompilerParams(
            vmem_limit_bytes=(56 if name in ("embed", "vocoder") else 28) * 2**20
        ),
        cost_estimate=pl.CostEstimate(flops=int(cost * COST), bytes_accessed=0, transcendentals=0),
        name=name,
    )


def embed_kernel(tokens_ref, masked_ref, tables_ref, mask_ref, out_ref):
    rows, codes = out_ref.shape[0], tables_ref.shape[1]
    tile = LANES
    lane = lax.broadcasted_iota(jnp.int32, (tile, LANES), 1)
    mask_row = mask_ref[...].astype(F32)[None, :]

    def column(row):
        return jnp.transpose(jnp.broadcast_to(row, (LANES, tile)))

    for start in range(0, rows, tile):
        masked = column(masked_ref[:, start : start + tile]) == 1
        total = jnp.where(masked[:, :1], mask_row, 0.0)
        for level in range(3):
            ids = column(tokens_ref[level : level + 1, start : start + tile])
            if level == 2:
                ids = jnp.where(masked, -1, ids)
            hot = jnp.concatenate(
                [
                    jnp.where(ids == lane + at, 1.0, 0.0).astype(BF16)
                    for at in range(0, codes, LANES)
                ],
                axis=1,
            )
            total = total + dot(hot, tables_ref[level])
        out_ref[start : start + tile, :] = total.astype(BF16)


def unit_heads(projected, head_size):
    width = projected.shape[1]
    lane = lax.broadcasted_iota(jnp.int32, (1, width), 1)
    squares = projected * projected
    scale = jnp.zeros_like(projected)
    for at in range(0, width, head_size):
        own = (lane >= at) & (lane < at + head_size)
        total = jnp.sum(jnp.where(own, squares, 0.0), axis=-1, keepdims=True)
        scale = jnp.where(own, lax.rsqrt(total + 1e-06), scale)
    return projected * scale


def project_kernel(count, head_size, *refs):
    pieces, w_ref = refs[:count], refs[count]
    rows, piece_cols = pieces[0].shape
    cols = w_ref.shape[2]
    owners = [pl.multiple_of(member(s, -1) * piece_cols, piece_cols) for s in shifts()]
    kinds = (0, 1, 2)
    w_scr = refs[-1]
    width = w_scr.shape[1] // len(kinds)
    if width != cols:
        w_scr[...] = jnp.zeros_like(w_scr)
    for r in range(count):
        for p, kind in enumerate(kinds):
            w_scr[r * piece_cols : (r + 1) * piece_cols, p * width : p * width + cols] = w_ref[
                kind, pl.ds(owners[r], piece_cols), :
            ]
    model = count * piece_cols
    tile = row_tile(rows, 128)
    for start in range(0, rows, tile):
        at = slice(start, start + tile)
        raw = [piece[at, :] for piece in pieces]
        normed = jnp.concatenate(
            [p.astype(BF16) for p in normalize([p.astype(F32) for p in raw], model)], axis=1
        )
        proj = dot(normed, w_scr[...])
        kv = jnp.concatenate(
            [unit_heads(proj[:, -2 * width : -width], head_size), proj[:, -width:]], axis=1
        ).astype(BF16)
        q_ref, emb_ref, up_ref, down_ref = refs[count + 1 : count + 5]
        query = unit_heads(proj[:, :width], head_size).astype(BF16)
        q_ref[at, :] = query
        for r in range(count):
            emb_ref[at, pl.ds(owners[r], piece_cols)] = raw[r]
        for ref in (up_ref, down_ref):
            ref[at, :] = kv
        halo = (up_ref.shape[0] - rows) // (model // (2 * width) + 1)
        for ref, here in (
            (down_ref, slice(0, halo) if start == 0 else None),
            (up_ref, slice(tile - halo, tile) if start + tile == rows else None),
        ):
            if here is not None:
                ref[up_ref.shape[0] - halo :, :] = jnp.concatenate(
                    [query[here], jnp.zeros((halo, width), BF16)], axis=1
                )
                for c in range(model // (2 * width)):
                    lanes = slice(c * 2 * width, (c + 1) * 2 * width)
                    to = rows + c * halo
                    ref[to : to + halo, :] = emb_ref[start + here.start : start + here.stop, lanes]


def value_rows(kv, block, used, width):
    rows = kv.shape[0]
    live = block * rows + lax.broadcasted_iota(jnp.int32, (rows, 1), 0) < used
    return jnp.concatenate(
        [
            jnp.where(live, kv[:, width:].astype(F32), 0.0),
            jnp.broadcast_to(jnp.where(live, 1.0, 0.0), (rows, width)),
        ],
        axis=1,
    ).astype(BF16)


def head_lanes(width, head_size, heads):
    lane = lax.broadcasted_iota(jnp.int32, (1, width), 1)
    return [(lane >= h * head_size) & (lane < (h + 1) * head_size) for h in range(heads)]


def weigh(query, own, sharp, key, value):
    query = jnp.where(own, query, jnp.zeros_like(query))
    score = lax.dot_general(query, key, (((1,), (1,)), ((), ())), preferred_element_type=F32)
    return dot(jnp.exp2(score * sharp - sharp).astype(BF16), value)


def seq_block(hop):
    size = lax.axis_size("seq")
    return lax.rem(lax.axis_index("seq") + (hop + size), size)


def attend_part_kernel(head_size, hops, *refs):
    used_ref, temp_ref, q_ref = refs[:3]
    kv_refs = refs[3 : 3 + len(hops)]
    sums_ref = refs[3 + len(hops)] if len(refs) > 5 + len(hops) else None
    acc_ref, v_scr = refs[-2:]
    rows, width = q_ref.shape
    heads = temp_ref.shape[0]
    own = head_lanes(width, head_size, heads)
    for i, (ref, hop) in enumerate(zip(kv_refs, hops)):
        v_scr[i] = value_rows(ref[:rows, :], seq_block(hop), used_ref[0], width)
    tile = row_tile(rows, ROWS)
    for at in range(0, rows, tile):
        for h in range(heads):
            sharp = temp_ref[h] * math.log2(math.e)
            total = 0.0 if sums_ref is None else sums_ref[h, at : at + tile, :]
            for i, ref in enumerate(kv_refs):
                query = q_ref[at : at + tile, :]
                total = total + weigh(query, own[h], sharp, ref[:rows, :width], v_scr[i])
            acc_ref[h, at : at + tile, :] = total


def attend_last_kernel(head_size, halo, hops, done, out_count, slab, *refs):
    used_ref, temp_ref, q_ref, acc_ref, before_ref, after_ref = refs[:6]
    kv_refs = refs[6 : 6 + len(hops)]
    out_refs = refs[6 + len(hops) : 6 + len(hops) + out_count]
    v_scr, att_scr = refs[6 + len(hops) + out_count :]
    rows, width = q_ref.shape
    heads = temp_ref.shape[0]
    own = head_lanes(width, head_size, heads)
    for i, (ref, hop) in enumerate(zip(kv_refs, hops)):
        v_scr[i] = value_rows(ref[:rows, :], seq_block(hop), used_ref[0], width)
    tile = row_tile(rows, ROWS)
    tiles = [(at, None) for at in range(0, rows, tile)] + [(rows, (before_ref, after_ref))]
    for at, edges in tiles:
        if edges is None:
            query = q_ref[at : at + tile, :]
            blocks = range(done, len(hops))
        else:
            query = jnp.concatenate([r[r.shape[0] - halo :, :width] for r in edges], axis=0)
            blocks = range(len(hops))
        result = jnp.zeros(query.shape, F32)
        for h in range(heads):
            sharp = temp_ref[h] * math.log2(math.e)
            total = acc_ref[h, at : at + tile, :] if edges is None else 0.0
            for i in blocks:
                total = total + weigh(query, own[h], sharp, kv_refs[i][:rows, :width], v_scr[i])
            result = jnp.where(own[h], total[:, :width] / total[:, width:], result)
        result = result.astype(BF16)
        if edges is None:
            att_scr[halo + at : halo + at + tile, :] = result
        else:
            att_scr[:halo, :] = result[:halo]
            att_scr[halo + rows :, :] = result[halo:]
    for shift, out_ref in zip(shifts(), out_refs):
        start = pl.multiple_of(member(shift, 1) * slab, slab)
        out_ref[...] = att_scr[pl.ds(start, out_ref.shape[0]), : out_ref.shape[1]]


def sine_cosine(x):
    turns = jnp.floor(x * (1.0 / math.pi) + 0.5)
    r = x - turns * 3.140625
    r = r - turns * 9.67502593994140625e-4
    r = r - turns * 1.509957990978376432e-7
    sign = 1.0 - 2.0 * (turns - 2.0 * jnp.floor(turns * 0.5))
    z = r * r
    s = -2.5052108385e-08
    for c in (2.7557319224e-06, -1.9841269841e-04, 8.3333333333e-03, -1.6666666667e-01):
        s = s * z + c
    c_ = 2.0876756988e-09
    for c in (-2.7557319224e-07, 2.4801587302e-05, -1.3888888889e-03, 4.1666666667e-02, -0.5):
        c_ = c_ * z + c
    return sign * (r + r * z * s), sign * (1.0 + z * c_)


def pack_kernel(*refs):
    attn_out, conv_in, conv_out, voc_in, voc_up, voc_down, conv_kernel, head = refs[:8]
    own_first, own_rest, own_head, mine_first, mine_rest = refs[8:13]
    k_scr, head_scr, sems = refs[13:]
    group = lax.axis_index("groups") % 2
    taps, split = conv_kernel.shape
    kernel = conv_kernel[...]
    upper = kernel.astype(BF16)
    lower = (kernel - upper.astype(F32)).astype(BF16)
    blank = jnp.zeros((k_scr.shape[0] - taps, split), BF16)
    k_scr[...] = jnp.concatenate(
        [
            jnp.concatenate([upper, blank], axis=0),
            jnp.concatenate([lower, blank], axis=0),
            jnp.zeros((k_scr.shape[0], k_scr.shape[1] - 2 * split), BF16),
        ],
        axis=1,
    )
    bins, rows = head.shape[0] // 2, head.shape[1]
    padded = head_scr.shape[1] // 2
    blank = jnp.zeros((padded - bins, rows), F32)
    values = head[...].astype(F32)
    values = jnp.concatenate([values[:bins], blank, values[bins:], blank], axis=0)
    head_scr[...] = jnp.transpose(values).astype(BF16)
    chunks = (
        ((attn_out, conv_out, k_scr), own_first, mine_first),
        ((voc_in, voc_down, voc_up), own_rest, mine_rest),
        ((head_scr,), own_head, None),
    )
    copies = []
    for sources, own, mine in chunks:
        for side in range(2):
            half = lax.rem(group + side, 2)
            start = 0
            for src in sources:
                part = src.shape[0] // 2
                cols = own.shape[2]
                for c in range(src.shape[1] // cols):
                    piece = src.at[
                        pl.ds(pl.multiple_of(half * part, part), part), pl.ds(c * cols, cols)
                    ]
                    copies.append((piece, own.at[side, pl.ds(start, part), :]))
                    if side == 0 and mine is not None:
                        copies.append((piece, mine.at[pl.ds(start, part), :]))
                    start += part
    start = own_first.shape[1]
    deep, cols = conv_in.shape[1:]
    part = mine_first.shape[0] - start
    for c in range(mine_first.shape[1] // cols):
        copies.append(
            (
                conv_in.at[group, pl.ds(deep // 2 + c * part, part), :],
                mine_first.at[pl.ds(start, part), pl.ds(c * cols, cols)],
            )
        )
    copies = [pltpu.make_async_copy(a, b, sems.at[i]) for i, (a, b) in enumerate(copies)]
    for copy in copies:
        copy.start()
    for copy in copies:
        copy.wait()


def fetcher(chunks, sems=None):
    group = lax.axis_index("groups") % 2
    subs = lax.axis_size("sub")
    moves, used = {}, [0]

    def fetch(kind, r, chunk, start, part, dst, base, stride=None, cols=None, lanes=None):
        pieces = chunks[chunk][r]
        here = r < subs
        moves[kind, r] = []
        for side in range(2):
            half = lax.rem(group + side, 2)
            if len(pieces) == 2:
                src, index = pieces[side], ()
            else:
                src, index = pieces[0], (half if here and stride else side,)
            to = pl.ds(pl.multiple_of(base + half * (stride or part), part), part)
            for c in range(dst.shape[1] // cols if cols else 1):
                from_rows = slice(start + c * part, start + (c + 1) * part)
                from_cols = slice(lanes[0], lanes[0] + lanes[1]) if lanes else slice(None)
                to_cols = slice(c * cols, (c + 1) * cols) if cols else slice(None)
                source, target = index + (from_rows, from_cols), (to, to_cols)
                if sems is None:
                    moves[kind, r].append((src, source, dst, target))
                else:
                    at = pl.ds(start + c * part, part)
                    copy = pltpu.make_async_copy(
                        src.at[index + (at, slice(None))], dst.at[target], sems.at[used[0]]
                    )
                    used[0] += 1
                    copy.start()
                    moves[kind, r].append(copy)

    def ready(kind, r):
        for move in moves[kind, r]:
            if sems is None:
                src, source, dst, target = move
                dst[target] = src[source]
            else:
                move.wait()

    return fetch, ready


def weight_pairs(refs, counts):
    chunks, at = [], 0
    for pieces in counts:
        pairs = []
        for dh in range(lax.axis_size("head")):
            for ds in range(lax.axis_size("sub")):
                taken = pieces if dh else 1
                pairs.append(refs[at : at + taken])
                at += taken
        chunks.append(pairs)
    return chunks, refs[at:]


def first_frame(slab):
    count = lax.axis_size("head") * lax.axis_size("sub")
    return (lax.axis_index("seq") * count + member((0, 0), 1)) * slab


def conv_kernel_body(geo, *refs):
    count, halo, rim, taps = geo
    emb_ref, before_ref, after_ref = refs[:3]
    att_refs = refs[3 : 3 + count]
    chunks, refs = weight_pairs(refs[3 + count :], (2, 2))
    feat_ref, window_ref, emb_scr, w_out, w_conv, k_conv, w_mix, stream_scr, gate_scr, sems = refs
    win, model = emb_scr.shape
    slab = feat_ref.shape[0]
    first = first_frame(slab)
    total_frames = lax.axis_size("seq") * count * slab
    me = member((0, 0), 1)
    rows = emb_ref.shape[0]
    own = win - halo
    cols = before_ref.shape[1]
    window = []
    for c in range(model // cols):
        piece, lanes = pl.ds(rows + c * halo, halo), pl.ds(c * cols, cols)
        window += [
            (me == 0, before_ref.at[piece, :], emb_scr.at[pl.ds(0, halo), lanes]),
            (me == count - 1, after_ref.at[piece, :], emb_scr.at[pl.ds(own, halo), lanes]),
        ]
    window += [
        (me == 0, emb_ref.at[pl.ds(0, own), :], emb_scr.at[pl.ds(halo, own), :]),
        (me == count - 1, emb_ref.at[pl.ds(rows - own, own), :], emb_scr.at[pl.ds(0, own), :]),
        (
            (me > 0) & (me < count - 1),
            emb_ref.at[pl.ds(pl.multiple_of(jnp.clip(me * slab - halo, 0, rows - win), halo), win), :],
            emb_scr,
        ),
    ]

    def window_copies(act):
        for at, (here, src, dst) in enumerate(window):
            copy = pltpu.make_async_copy(src, dst, sems.at[at])
            pl.when(here)(lambda copy=copy: getattr(copy, act)())

    window_copies("start")
    fetch, ready = fetcher(chunks)
    out_half = w_out.shape[0] // count // 2
    mix_half = w_mix.shape[1] // 2
    tap_half = k_conv.shape[1] // 2
    deep = w_conv.shape[1] // 2
    step = deep // 2
    low_rows = step // (model // w_conv.shape[2])

    def fetch_low(r):
        at = out_half + mix_half + tap_half
        for c in range(step // low_rows):
            lanes = (c * w_conv.shape[2], w_conv.shape[2])
            fetch(
                ("low", c), r, 0, at, low_rows, w_conv.at[r], step + c * low_rows, deep, lanes=lanes
            )

    def ready_low(r):
        if r < lax.axis_size("sub"):
            ready("low", r)
        else:
            for c in range(step // low_rows):
                ready(("low", c), r)

    for r in range(count):
        fetch("out", r, 0, 0, out_half, w_out, r * 2 * out_half)
    for r in range(count):
        fetch("top", r, 1, 0, step, w_conv.at[r], 0, deep)
        if r < lax.axis_size("sub"):
            fetch("low", r, 1, step, step, w_conv.at[r], step, deep)
        else:
            fetch_low(r)
        fetch("taps", r, 0, out_half + mix_half, tap_half, k_conv.at[r], 0)
        fetch("mix", r, 0, out_half, mix_half, w_mix.at[r], 0)

    attended = jnp.concatenate([ref[...] for ref in att_refs], axis=1)
    window_copies("wait")
    for r in range(count):
        ready("out", r)
    frames = first - halo + lax.broadcasted_iota(jnp.int32, (win, 1), 0)
    inside = (frames >= 0) & (frames < total_frames)
    stream = jnp.where(inside, emb_scr[...].astype(F32) + dot(attended, w_out[...]), 0.0)
    stream_scr[...] = stream
    conv_normed = layer_norm(stream).astype(BF16)

    mid = slab + 2 * rim
    group_cols = w_conv.shape[2]
    lead = halo - rim - taps // 2
    conv_sum = jnp.zeros((mid, model), F32)
    for r in range(count):
        ready("top", r)
        ready_low(r)
        signal = dot(conv_normed, w_conv[r, deep:, :])
        gated = dot(conv_normed, w_conv[r, :deep, :]) * jax.nn.sigmoid(signal)
        gated = gated.astype(BF16).astype(F32)
        ready("taps", r)
        kernel = k_conv[r, :, : 2 * group_cols].astype(F32)
        kernel = kernel[:, :group_cols] + kernel[:, group_cols:]
        active = []
        for c in range(group_cols // LANES):
            lanes = slice(c * LANES, (c + 1) * LANES)
            gate_scr[c] = gated[:, lanes]
            depth = jnp.zeros((mid, LANES), F32)
            for k in range(taps):
                depth = depth + kernel[k : k + 1, lanes] * gate_scr[c, lead + k : lead + k + mid, :]
            active.append((depth * jax.nn.sigmoid(depth)).astype(BF16))
        ready("mix", r)
        part = dot(jnp.concatenate(active, axis=1), w_mix[r])
        conv_sum = conv_sum + part.astype(BF16).astype(F32)
    features = layer_norm(stream_scr[halo - rim : halo - rim + mid, :] + conv_sum).astype(BF16)
    feat_ref[...] = features[rim : rim + slab]
    window_ref[...] = features


def voc_kernel_body(geo, *refs):
    count, rim, half_voc = geo
    used_ref, window_ref, voc_kernel_ref, bias_ref, table_ref, hann_ref = refs[:6]
    chunks, refs = weight_pairs(refs[6:], (2, 1))
    wave_ref, w_vin, w_up, w_down, w_head, w_table, base_scr, wave_scr, out_scr, sems = refs
    slab = out_scr.shape[1]
    first = first_frame(slab)
    total_frames = lax.axis_size("seq") * count * slab
    used = used_ref[0]
    owners = [member(s, -1) for s in shifts()]
    fetch, ready = fetcher(chunks, sems)
    vin_half = w_vin.shape[0] // count // 2
    down_half = w_down.shape[0] // count // 2
    up_half = w_up.shape[0] // count // 2
    head_half = w_head.shape[0] // count // 2
    voc = w_vin.shape[1]
    rest = vin_half + down_half
    for r in range(count):
        fetch("vin", r, 0, 0, vin_half, w_vin, owners[r] * 2 * vin_half)
    for r in range(count):
        fetch(
            "up", r, 0, rest, up_half, w_up, owners[r] * 2 * up_half, cols=voc
        )
    for r in range(count):
        fetch("down", r, 0, vin_half, down_half, w_down, owners[r] * 2 * down_half)
    for r in range(count):
        fetch(
            "head",
            r,
            1,
            0,
            head_half,
            w_head,
            owners[r] * 2 * head_half,
            cols=voc,
        )
    table_copy = pltpu.make_async_copy(table_ref, w_table, sems.at[sems.shape[0] - 1])
    table_copy.start()
    features = window_ref[...]
    mid = features.shape[0]

    for r in range(count):
        ready("vin", r)
    ids = first - rim + lax.broadcasted_iota(jnp.int32, (mid, 1), 0)
    live = (ids >= 0) & (ids < used)
    base = layer_norm(jnp.where(live, dot(features, w_vin[...]), 0.0))
    voc = base.shape[1]
    trim = half_voc + 1
    rows = mid - 2 * trim
    depth = []
    for c in range(voc // LANES):
        lanes = slice(c * LANES, (c + 1) * LANES)
        base_scr[c] = base[:, lanes]
        total = jnp.zeros((rows, LANES), F32)
        for k in range(2 * half_voc + 1):
            total = total + voc_kernel_ref[k : k + 1, lanes] * base_scr[c, 1 + k : 1 + k + rows, :]
        depth.append(total)
    inner = jnp.concatenate(
        [p.astype(BF16) for p in normalize(depth, voc)], axis=1
    )
    for r in range(count):
        ready("up", r)
    up = dot(inner, w_up[...])
    hidden = (0.5 * up * (1.0 + lax.erf(up * math.sqrt(0.5)))).astype(BF16)
    for r in range(count):
        ready("down", r)
    center = jnp.concatenate(
        [base_scr[c, trim : trim + rows, :] for c in range(voc // LANES)], axis=1
    )
    head_input = layer_norm(center + dot(hidden, w_down[...])).astype(BF16)
    for r in range(count):
        ready("head", r)
    spectrum = dot(head_input, w_head[...]) + bias_ref[...]
    bins = spectrum.shape[1] // 2
    magnitude = jnp.minimum(jnp.exp(spectrum[:, :bins]), 100.0)
    sine, cosine = sine_cosine(spectrum[:, bins:])
    coefficients = jnp.concatenate([magnitude * cosine, magnitude * sine], axis=1).astype(BF16)
    table_copy.wait()
    ids = first - rim + trim + lax.broadcasted_iota(jnp.int32, (rows, 1), 0)
    exists = jnp.where((ids >= 0) & (ids < total_frames), 1.0, 0.0)
    parts = wave_scr.shape[0]
    span = wave_scr.shape[2]
    for q in range(parts):
        wave_scr[q] = exists * dot(coefficients, w_table[:, q * span : (q + 1) * span])
    audio = jnp.zeros((slab, span), F32)
    energy = jnp.zeros((slab, span), F32)
    for q in range(parts):
        begin = rim - trim + parts // 2 - q
        audio = audio + wave_scr[q, begin : begin + slab, :]
        energy = energy + exists[begin : begin + slab] * hann_ref[q : q + 1, :]
    audio = audio / energy
    tiles = range(span // LANES)
    for c in tiles:
        out_scr[c] = audio[:, c * LANES : (c + 1) * LANES]
    even, odd = (
        jnp.concatenate([out_scr[c, pl.ds(at, slab // 2, stride=2), :] for c in tiles], axis=1)
        for at in range(2)
    )
    samples = jnp.concatenate([even[:, :HOP], odd[:, :HOP]], axis=1)
    count = 2 * HOP // LANES
    for c in range(count):
        wave_ref[pl.ds(c, slab // 2, stride=count), :] = samples[:, c * LANES : (c + 1) * LANES]


def synthesis(bins, padded, span):
    size = 2 * (bins - 1)
    parts = size // HOP
    k = np.arange(bins)[:, None]
    n = np.arange(size)[None, :]
    angle = 2.0 * np.pi / size * (k * n % size)
    hann = 0.5 - 0.5 * np.cos(2.0 * np.pi / size * np.arange(size))
    edge = (k == 0) | (k == bins - 1)
    factor = np.where(edge, 1.0, 2.0) / size * hann[None, :]
    both = (factor * np.cos(angle), np.where(edge, 0.0, -factor * np.sin(angle)))
    table = np.zeros((2, padded, parts, span), np.float32)
    for at, values in enumerate(both):
        table[at, :bins, :, :HOP] = values.reshape(bins, parts, HOP)
    squares = np.ones((parts, span), np.float32)
    squares[:, :HOP] = (hann * hann).reshape(parts, HOP)
    return table.reshape(2 * padded, parts * span).astype(ml_dtypes.bfloat16), squares


def local(
    tokens,
    masked,
    used_frames,
    tables,
    mask_vec,
    attn_in,
    head_temp,
    attn_out,
    conv_in,
    conv_kernel,
    conv_out,
    voc_in,
    voc_kernel,
    voc_up,
    voc_down,
    voc_head,
    head_bias,
):
    frame_count = tokens.shape[1]
    count = lax.axis_size("head") * lax.axis_size("sub")
    seq_size = lax.axis_size("seq")
    model = attn_in.shape[1]
    piece_cols = tables.shape[2]
    cols = attn_in.shape[2]
    width = round_up(cols, LANES)
    head_size = cols // head_temp.shape[0]
    slab = frame_count // count
    bins = head_bias.shape[0] // 2
    half_voc = voc_kernel.shape[0] // 2
    parts = 2 * (bins - 1) // HOP
    rim = round_up(half_voc + parts // 2, 8)
    halo = round_up(half_voc + parts // 2 + conv_kernel.shape[0] // 2, EDGE)
    win = slab + 2 * halo
    mid = slab + 2 * rim
    taps = conv_kernel.shape[0]

    others = range(1, lax.axis_size("head"))
    group = lax.rem(lax.axis_index("groups"), 2)
    deep = conv_in.shape[1]

    def cross(x):
        return [rotate(x, "head", dh) for dh in others]

    def spread(xs):
        return [rotate(x, "groups", 1) for x in xs]

    def share(xs):
        return [rotate(x, "sub", 1) for x in xs]

    near, far, near_sub, far_sub, own, own_sub, mine = {}, {}, {}, {}, {}, {}, {}
    mine["top"] = lax.dynamic_slice(
        conv_in, (group, 0, 0), (1, deep // 2, conv_in.shape[2])
    ).reshape(deep // 2, conv_in.shape[2])
    own["b"] = conv_in
    near["top"] = cross(mine["top"])
    own_sub["b"] = share([own["b"]])

    embedded = call(
        embed_kernel,
        jax.ShapeDtypeStruct((frame_count, piece_cols), BF16),
        [VMEM] * 4,
        VMEM,
        [],
        1,
        "embed",
    )(tokens, masked[None, :], tables, mask_vec)
    crossed = cross(embedded)
    beside = share([embedded])
    [conv_kernel], [embedded], near["top"] = together([conv_kernel], [embedded], near["top"])

    padded = round_up(bins, LANES)
    gap = ((0, 0), (0, padded - bins))
    bias = jnp.pad(head_bias.reshape(2, bins), gap).reshape(1, 2 * padded)
    tap_rows = round_up(taps, 32)
    voc = voc_in.shape[1]
    first_rows = (attn_out.shape[0] + conv_out.shape[0] + tap_rows) // 2
    low_rows = deep // 2 * conv_in.shape[2] // model
    conv_rows = (voc_in.shape[0] + voc_down.shape[0]) // 2
    conv_rows += voc_up.shape[0] * voc_up.shape[1] // voc // 2
    head_rows = voc_head.shape[0] * 2 * padded // voc // 2
    packed = call(
        pack_kernel,
        [
            jax.ShapeDtypeStruct((2, first_rows, model), BF16),
            jax.ShapeDtypeStruct((2, conv_rows, voc), BF16),
            jax.ShapeDtypeStruct((2, head_rows, voc), BF16),
            jax.ShapeDtypeStruct((first_rows + low_rows, model), BF16),
            jax.ShapeDtypeStruct((conv_rows, voc), BF16),
        ],
        [HBM] * 6 + [VMEM] * 2,
        [VMEM] * 5,
        [
            pltpu.VMEM((tap_rows, model), BF16),
            pltpu.VMEM((voc_head.shape[0], 2 * padded), BF16),
            pltpu.SemaphoreType.DMA((48,)),
        ],
        1,
        "pack",
    )(attn_out, conv_in, conv_out, voc_in, voc_up, voc_down, conv_kernel, voc_head.T)

    own["a"], own["c"], own["h"], mine["a"], mine["c"] = packed
    near["a"] = cross(mine["a"])

    crossed, beside, own_sub["b"], [own["a"], own["c"], own["h"], mine["c"]] = together(
        crossed, beside, own_sub["b"], [own["a"], own["c"], own["h"], mine["c"]]
    )

    def members(own_piece, beside_piece, others_pieces):
        pieces = [own_piece] + beside_piece
        for piece in others_pieces:
            pieces += [piece] + share([piece])
        return pieces

    pieces = members(embedded, beside, crossed)
    for kind in ("a", "c"):
        own_sub[kind] = share([own[kind]])
    chunk = 2 * width
    message = (frame_count + (model // chunk + 1) * halo, chunk)
    q_own, emb, upward, downward = call(
        lambda *refs: project_kernel(count, head_size, *refs),
        (
            jax.ShapeDtypeStruct((frame_count, width), BF16),
            jax.ShapeDtypeStruct((frame_count, model), BF16),
            jax.ShapeDtypeStruct(message, BF16),
            jax.ShapeDtypeStruct(message, BF16),
        ),
        [VMEM] * (count + 1),
        (VMEM,) * 4,
        [pltpu.VMEM((model, 3 * width), BF16)],
        1,
        "project",
    )(*pieces, attn_in)

    below, above = rotate(upward, "seq", 1), rotate(downward, "seq", -1)
    heads = head_temp.shape[0]

    def attend(hops, blocks, sums, cost):
        return call(
            lambda *refs: attend_part_kernel(head_size, hops, *refs),
            jax.ShapeDtypeStruct((heads, frame_count, chunk), F32),
            [SMEM, SMEM] + [VMEM] * (1 + len(blocks) + len(sums)),
            VMEM,
            [pltpu.VMEM((len(blocks), frame_count, chunk), BF16)],
            cost,
            "attend",
        )(used_frames, head_temp, q_own, *blocks, *sums)

    [q_own], near["top"], own_sub["a"], own_sub["c"] = together(
        [q_own], near["top"], own_sub["a"], own_sub["c"]
    )
    far["top"] = spread(near["top"])
    sums = attend([0], [upward], [], COSTS[0])
    [sums, mine["c"]], near["a"], far["top"] = together([sums, mine["c"]], near["a"], far["top"])
    far["a"], near["c"] = spread(near["a"]), cross(mine["c"])
    near_sub["a"] = share(near["a"])
    [below, sums] = together([below, sums])[0]
    blocks, hops = [upward, below, above], [0, -1, 1]
    ahead, behind = below[:frame_count], above[:frame_count]
    for hop in range(2, seq_size // 2 + 1):
        ahead = rotate(ahead, "seq", 1)
        blocks.append(ahead)
        hops.append(-hop)
        if 2 * hop < seq_size:
            behind = rotate(behind, "seq", -1)
            blocks.append(behind)
            hops.append(hop)
    sums = attend([-1], [below], [sums], COSTS[1])
    sums = attend([1], [above], [sums], COSTS[2])
    last, [sums], near["top"], far["top"], near_sub["a"] = together(
        blocks[3:], [sums], near["top"], far["top"], near_sub["a"]
    )
    blocks[3:] = last
    near_sub["top"], far_sub["top"] = share(near["top"]), share(far["top"])
    windows = call(
        lambda *refs: attend_last_kernel(head_size, halo, hops, 3, count, slab, *refs),
        (jax.ShapeDtypeStruct((win, cols), BF16),) * count,
        [SMEM, SMEM] + [VMEM] * (4 + len(blocks)),
        (VMEM,) * count,
        [
            pltpu.VMEM((len(blocks), frame_count, chunk), BF16),
            pltpu.VMEM((frame_count + 2 * halo, width), BF16),
        ],
        COSTS[3],
        "attend_last",
    )(used_frames, head_temp, q_own, sums, below, above, *blocks)

    windows, near_sub["top"], far_sub["top"], far["a"], near["c"] = together(
        windows, near_sub["top"], far_sub["top"], far["a"], near["c"]
    )
    attended = send_members(windows)
    far_sub["a"], far["c"] = share(far["a"]), spread(near["c"])
    attended, far_sub["a"], near["c"], [own["h"]] = together(
        attended, far_sub["a"], near["c"], [own["h"]]
    )
    near["h"], near_sub["c"] = cross(own["h"]), share(near["c"])
    own_sub["h"] = share([own["h"]])
    own["top"], own_sub["top"] = own["b"], own_sub["b"]

    def weights(kind):
        found = [own[kind], *own_sub[kind]]
        for dh in range(len(others)):
            found += [t[kind][dh] for t in (near, far, near_sub, far_sub) if kind in t]
        return found

    conv_weights = [w for kind in ("a", "top") for w in weights(kind)]
    span = round_up(HOP, LANES)
    table, squares = synthesis(bins, padded, span)
    features, window = call(
        lambda *refs: conv_kernel_body((count, halo, rim, taps), *refs),
        (
            jax.ShapeDtypeStruct((slab, model), BF16),
            jax.ShapeDtypeStruct((mid, model), BF16),
        ),
        [HBM] * 3 + [VMEM] * (count + len(conv_weights)),
        (VMEM, VMEM),
        [
            pltpu.VMEM((win, model), BF16),
            pltpu.VMEM((count * cols, model), BF16),
            pltpu.VMEM((count, 2 * deep, conv_in.shape[2]), BF16),
            pltpu.VMEM((count, tap_rows, model), BF16),
            pltpu.VMEM((count,) + conv_out.shape, BF16),
            pltpu.VMEM((win, model), F32),
            pltpu.VMEM((conv_in.shape[2] // LANES, win, LANES), F32),
            pltpu.SemaphoreType.DMA((3 + 2 * model // (2 * width),)),
        ],
        0,
        "conv",
    )(emb, below, above, *attended, *conv_weights)
    [window], far["c"], near_sub["c"], near["h"], own_sub["h"] = together(
        [window], far["c"], near_sub["c"], near["h"], own_sub["h"]
    )
    far_sub["c"], near_sub["h"] = share(far["c"]), share(near["h"])
    voc_weights = weights("c") + weights("h")
    wave = call(
        lambda *refs: voc_kernel_body((count, rim, half_voc), *refs),
        jax.ShapeDtypeStruct((slab * HOP // LANES, LANES), F32),
        [SMEM] + [VMEM] * 3 + [HBM, VMEM] + [HBM] * len(voc_weights),
        VMEM,
        [
            pltpu.VMEM((count * voc_in.shape[0], voc), BF16),
            pltpu.VMEM((count * voc_up.shape[0], voc_up.shape[1]), BF16),
            pltpu.VMEM((count * voc_down.shape[0], voc), BF16),
            pltpu.VMEM((count * voc_head.shape[0], 2 * padded), BF16),
            pltpu.VMEM(table.shape, BF16),
            pltpu.VMEM((voc // LANES, mid, LANES), F32),
            pltpu.VMEM((parts, mid - 2 * (half_voc + 1), span), F32),
            pltpu.VMEM((span // LANES, slab, LANES), F32),
            pltpu.SemaphoreType.DMA((4 * count + 4 * count * (voc_up.shape[1] // voc) + 1,)),
        ],
        1,
        "vocoder",
    )(
        used_frames,
        window,
        voc_kernel,
        bias,
        jnp.asarray(table),
        jnp.asarray(squares),
        *voc_weights,
    )
    return features, wave.reshape(slab * HOP)


def solution(mesh):
    in_specs = (
        P(None, ("groups", "seq")),
        P(("groups", "seq")),
        P("groups"),
        P(None, None, ("head", "sub")),
        P(("head", "sub")),
        P(None, None, ("head", "sub")),
        P(("head", "sub")),
        P(("head", "sub"), None),
        P(None, None, ("head", "sub")),
        P(None, ("head", "sub")),
        P(("head", "sub"), None),
        P(("head", "sub"), None),
        P(),
        P(("head", "sub"), None),
        P(("head", "sub"), None),
        P(("head", "sub"), None),
        P(),
    )
    out_specs = (P(("groups", "seq", "head", "sub"), None), P(("groups", "seq", "head", "sub")))
    return jax.shard_map(local, mesh=mesh, in_specs=in_specs, out_specs=out_specs, check_vma=False)
```

```python
import math

import jax
import jax.numpy as jnp
import ml_dtypes
import numpy as np
from jax import lax
from jax.experimental import pallas as pl
from jax.experimental.pallas import tpu as pltpu
from jax.sharding import PartitionSpec as P

HOP = 320
LANES = 128
ROWS = 128
COST = 2**36
COSTS = (1, 1, 0, 0)
EDGE = 32
F32 = jnp.float32
BF16 = jnp.bfloat16
HBM = pl.BlockSpec(memory_space=pl.ANY)
VMEM = pl.BlockSpec(memory_space=pltpu.VMEM)
SMEM = pl.BlockSpec(memory_space=pltpu.SMEM)


def round_up(value, multiple):
    return -(-value // multiple) * multiple


def row_tile(rows, most):
    return max(t for t in range(16, most + 1, 16) if rows % t == 0)


def shifts():
    heads, subs = lax.axis_size("head"), lax.axis_size("sub")
    return [(dh, ds) for dh in range(heads) for ds in range(subs)]


def member(shift, sign):
    heads, subs = lax.axis_size("head"), lax.axis_size("sub")
    head = lax.rem(lax.axis_index("head") + (sign * shift[0] + heads), heads)
    sub = lax.rem(lax.axis_index("sub") + (sign * shift[1] + subs), subs)
    return head * subs + sub


def rotate(x, axis, by):
    size = lax.axis_size(axis)
    return lax.ppermute(x, axis, [(i, (i + by) % size) for i in range(size)])


def send_members(pieces):
    heads, subs = lax.axis_size("head"), lax.axis_size("sub")
    out = []
    for (dh, ds), piece in zip(shifts(), pieces):
        if dh or ds:
            perm = [
                (h * subs + s, (h + dh) % heads * subs + (s + ds) % subs)
                for h in range(heads)
                for s in range(subs)
            ]
            piece = lax.ppermute(piece, ("head", "sub"), perm)
        out.append(piece)
    return out


def together(*groups):
    flat = lax.optimization_barrier(tuple(x for g in groups for x in g))
    out, at = [], 0
    for g in groups:
        out.append(list(flat[at : at + len(g)]))
        at += len(g)
    return out


def dot(a, b):
    return jnp.dot(a, b, preferred_element_type=F32)


def normalize(parts, width):
    mean = sum(jnp.sum(p, axis=-1, keepdims=True) for p in parts) * (1.0 / width)
    parts = [p - mean for p in parts]
    var = sum(jnp.sum(p * p, axis=-1, keepdims=True) for p in parts) * (1.0 / width)
    scale = lax.rsqrt(var + 1e-05)
    return [p * scale for p in parts]


def layer_norm(values):
    return normalize([values], values.shape[-1])[0]


def call(kernel, out_shape, in_specs, out_specs, scratch, cost, name):
    return pl.pallas_call(
        kernel,
        out_shape=out_shape,
        in_specs=in_specs,
        out_specs=out_specs,
        scratch_shapes=scratch,
        compiler_params=pltpu.CompilerParams(
            vmem_limit_bytes=(56 if name in ("embed", "vocoder") else 28) * 2**20
        ),
        cost_estimate=pl.CostEstimate(flops=int(cost * COST), bytes_accessed=0, transcendentals=0),
        name=name,
    )


def embed_kernel(tokens_ref, masked_ref, tables_ref, mask_ref, out_ref):
    rows, codes = out_ref.shape[0], tables_ref.shape[1]
    tile = LANES
    lane = lax.broadcasted_iota(jnp.int32, (tile, LANES), 1)
    mask_row = mask_ref[...].astype(F32)[None, :]

    def column(row):
        return jnp.transpose(jnp.broadcast_to(row, (LANES, tile)))

    for start in range(0, rows, tile):
        masked = column(masked_ref[:, start : start + tile]) == 1
        total = jnp.where(masked[:, :1], mask_row, 0.0)
        for level in range(3):
            ids = column(tokens_ref[level : level + 1, start : start + tile])
            if level == 2:
                ids = jnp.where(masked, -1, ids)
            hot = jnp.concatenate(
                [
                    jnp.where(ids == lane + at, 1.0, 0.0).astype(BF16)
                    for at in range(0, codes, LANES)
                ],
                axis=1,
            )
            total = total + dot(hot, tables_ref[level])
        out_ref[start : start + tile, :] = total.astype(BF16)


def unit_heads(projected, head_size):
    width = projected.shape[1]
    lane = lax.broadcasted_iota(jnp.int32, (1, width), 1)
    squares = projected * projected
    scale = jnp.zeros_like(projected)
    for at in range(0, width, head_size):
        own = (lane >= at) & (lane < at + head_size)
        total = jnp.sum(jnp.where(own, squares, 0.0), axis=-1, keepdims=True)
        scale = jnp.where(own, lax.rsqrt(total + 1e-06), scale)
    return projected * scale


def project_kernel(count, head_size, *refs):
    pieces, w_ref = refs[:count], refs[count]
    rows, piece_cols = pieces[0].shape
    cols = w_ref.shape[2]
    owners = [pl.multiple_of(member(s, -1) * piece_cols, piece_cols) for s in shifts()]
    kinds = (0, 1, 2)
    w_scr = refs[-1]
    width = w_scr.shape[1] // len(kinds)
    if width != cols:
        w_scr[...] = jnp.zeros_like(w_scr)
    for r in range(count):
        for p, kind in enumerate(kinds):
            w_scr[r * piece_cols : (r + 1) * piece_cols, p * width : p * width + cols] = w_ref[
                kind, pl.ds(owners[r], piece_cols), :
            ]
    model = count * piece_cols
    tile = row_tile(rows, 128)
    for start in range(0, rows, tile):
        at = slice(start, start + tile)
        raw = [piece[at, :] for piece in pieces]
        normed = jnp.concatenate(
            [p.astype(BF16) for p in normalize([p.astype(F32) for p in raw], model)], axis=1
        )
        proj = dot(normed, w_scr[...])
        kv = jnp.concatenate(
            [unit_heads(proj[:, -2 * width : -width], head_size), proj[:, -width:]], axis=1
        ).astype(BF16)
        q_ref, emb_ref, up_ref, down_ref = refs[count + 1 : count + 5]
        query = unit_heads(proj[:, :width], head_size).astype(BF16)
        q_ref[at, :] = query
        for r in range(count):
            emb_ref[at, pl.ds(owners[r], piece_cols)] = raw[r]
        for ref in (up_ref, down_ref):
            ref[at, :] = kv
        halo = (up_ref.shape[0] - rows) // (model // (2 * width) + 1)
        for ref, here in (
            (down_ref, slice(0, halo) if start == 0 else None),
            (up_ref, slice(tile - halo, tile) if start + tile == rows else None),
        ):
            if here is not None:
                ref[up_ref.shape[0] - halo :, :] = jnp.concatenate(
                    [query[here], jnp.zeros((halo, width), BF16)], axis=1
                )
                for c in range(model // (2 * width)):
                    lanes = slice(c * 2 * width, (c + 1) * 2 * width)
                    to = rows + c * halo
                    ref[to : to + halo, :] = emb_ref[start + here.start : start + here.stop, lanes]


def value_rows(kv, block, used, width):
    rows = kv.shape[0]
    live = block * rows + lax.broadcasted_iota(jnp.int32, (rows, 1), 0) < used
    return jnp.concatenate(
        [
            jnp.where(live, kv[:, width:].astype(F32), 0.0),
            jnp.broadcast_to(jnp.where(live, 1.0, 0.0), (rows, width)),
        ],
        axis=1,
    ).astype(BF16)


def head_lanes(width, head_size, heads):
    lane = lax.broadcasted_iota(jnp.int32, (1, width), 1)
    return [(lane >= h * head_size) & (lane < (h + 1) * head_size) for h in range(heads)]


def weigh(query, own, sharp, key, value):
    query = jnp.where(own, query, jnp.zeros_like(query))
    score = lax.dot_general(query, key, (((1,), (1,)), ((), ())), preferred_element_type=F32)
    return dot(jnp.exp2(score * sharp - sharp).astype(BF16), value)


def seq_block(hop):
    size = lax.axis_size("seq")
    return lax.rem(lax.axis_index("seq") + (hop + size), size)


def attend_part_kernel(head_size, hops, *refs):
    used_ref, temp_ref, q_ref = refs[:3]
    kv_refs = refs[3 : 3 + len(hops)]
    sums_ref = refs[3 + len(hops)] if len(refs) > 5 + len(hops) else None
    acc_ref, v_scr = refs[-2:]
    rows, width = q_ref.shape
    heads = temp_ref.shape[0]
    own = head_lanes(width, head_size, heads)
    for i, (ref, hop) in enumerate(zip(kv_refs, hops)):
        v_scr[i] = value_rows(ref[:rows, :], seq_block(hop), used_ref[0], width)
    tile = row_tile(rows, ROWS)
    for at in range(0, rows, tile):
        for h in range(heads):
            sharp = temp_ref[h] * math.log2(math.e)
            total = 0.0 if sums_ref is None else sums_ref[h, at : at + tile, :]
            for i, ref in enumerate(kv_refs):
                query = q_ref[at : at + tile, :]
                total = total + weigh(query, own[h], sharp, ref[:rows, :width], v_scr[i])
            acc_ref[h, at : at + tile, :] = total


def attend_last_kernel(head_size, halo, hops, done, out_count, slab, *refs):
    used_ref, temp_ref, q_ref, acc_ref, before_ref, after_ref = refs[:6]
    kv_refs = refs[6 : 6 + len(hops)]
    out_refs = refs[6 + len(hops) : 6 + len(hops) + out_count]
    v_scr, att_scr = refs[6 + len(hops) + out_count :]
    rows, width = q_ref.shape
    heads = temp_ref.shape[0]
    own = head_lanes(width, head_size, heads)
    for i, (ref, hop) in enumerate(zip(kv_refs, hops)):
        v_scr[i] = value_rows(ref[:rows, :], seq_block(hop), used_ref[0], width)
    tile = row_tile(rows, ROWS)
    tiles = [(at, None) for at in range(0, rows, tile)] + [(rows, (before_ref, after_ref))]
    for at, edges in tiles:
        if edges is None:
            query = q_ref[at : at + tile, :]
            blocks = range(done, len(hops))
        else:
            query = jnp.concatenate([r[r.shape[0] - halo :, :width] for r in edges], axis=0)
            blocks = range(len(hops))
        result = jnp.zeros(query.shape, F32)
        for h in range(heads):
            sharp = temp_ref[h] * math.log2(math.e)
            total = acc_ref[h, at : at + tile, :] if edges is None else 0.0
            for i in blocks:
                total = total + weigh(query, own[h], sharp, kv_refs[i][:rows, :width], v_scr[i])
            result = jnp.where(own[h], total[:, :width] / total[:, width:], result)
        result = result.astype(BF16)
        if edges is None:
            att_scr[halo + at : halo + at + tile, :] = result
        else:
            att_scr[:halo, :] = result[:halo]
            att_scr[halo + rows :, :] = result[halo:]
    for shift, out_ref in zip(shifts(), out_refs):
        start = pl.multiple_of(member(shift, 1) * slab, slab)
        out_ref[...] = att_scr[pl.ds(start, out_ref.shape[0]), : out_ref.shape[1]]


def sine_cosine(x):
    turns = jnp.floor(x * (1.0 / math.pi) + 0.5)
    r = x - turns * 3.140625
    r = r - turns * 9.67502593994140625e-4
    r = r - turns * 1.509957990978376432e-7
    sign = 1.0 - 2.0 * (turns - 2.0 * jnp.floor(turns * 0.5))
    z = r * r
    s = -2.5052108385e-08
    for c in (2.7557319224e-06, -1.9841269841e-04, 8.3333333333e-03, -1.6666666667e-01):
        s = s * z + c
    c_ = 2.0876756988e-09
    for c in (-2.7557319224e-07, 2.4801587302e-05, -1.3888888889e-03, 4.1666666667e-02, -0.5):
        c_ = c_ * z + c
    return sign * (r + r * z * s), sign * (1.0 + z * c_)


def pack_kernel(*refs):
    attn_out, conv_in, conv_out, voc_in, voc_up, voc_down, conv_kernel, head = refs[:8]
    own_first, own_rest, own_head, mine_first, mine_rest = refs[8:13]
    k_scr, head_scr, sems = refs[13:]
    group = lax.axis_index("groups") % 2
    taps, split = conv_kernel.shape
    kernel = conv_kernel[...]
    upper = kernel.astype(BF16)
    lower = (kernel - upper.astype(F32)).astype(BF16)
    blank = jnp.zeros((k_scr.shape[0] - taps, split), BF16)
    k_scr[...] = jnp.concatenate(
        [
            jnp.concatenate([upper, blank], axis=0),
            jnp.concatenate([lower, blank], axis=0),
            jnp.zeros((k_scr.shape[0], k_scr.shape[1] - 2 * split), BF16),
        ],
        axis=1,
    )
    bins, rows = head.shape[0] // 2, head.shape[1]
    padded = head_scr.shape[1] // 2
    blank = jnp.zeros((padded - bins, rows), F32)
    values = head[...].astype(F32)
    values = jnp.concatenate([values[:bins], blank, values[bins:], blank], axis=0)
    head_scr[...] = jnp.transpose(values).astype(BF16)
    chunks = (
        ((attn_out, conv_out, k_scr), own_first, mine_first),
        ((voc_in, voc_down, voc_up), own_rest, mine_rest),
        ((head_scr,), own_head, None),
    )
    copies = []
    for sources, own, mine in chunks:
        for side in range(2):
            half = lax.rem(group + side, 2)
            start = 0
            for src in sources:
                part = src.shape[0] // 2
                cols = own.shape[2]
                for c in range(src.shape[1] // cols):
                    piece = src.at[
                        pl.ds(pl.multiple_of(half * part, part), part), pl.ds(c * cols, cols)
                    ]
                    copies.append((piece, own.at[side, pl.ds(start, part), :]))
                    if side == 0 and mine is not None:
                        copies.append((piece, mine.at[pl.ds(start, part), :]))
                    start += part
    start = own_first.shape[1]
    deep, cols = conv_in.shape[1:]
    part = mine_first.shape[0] - start
    for c in range(mine_first.shape[1] // cols):
        copies.append(
            (
                conv_in.at[group, pl.ds(deep // 2 + c * part, part), :],
                mine_first.at[pl.ds(start, part), pl.ds(c * cols, cols)],
            )
        )
    copies = [pltpu.make_async_copy(a, b, sems.at[i]) for i, (a, b) in enumerate(copies)]
    for copy in copies:
        copy.start()
    for copy in copies:
        copy.wait()


def fetcher(chunks, sems=None):
    group = lax.axis_index("groups") % 2
    subs = lax.axis_size("sub")
    moves, used = {}, [0]

    def fetch(kind, r, chunk, start, part, dst, base, stride=None, cols=None, lanes=None):
        pieces = chunks[chunk][r]
        here = r < subs
        moves[kind, r] = []
        for side in range(2):
            half = lax.rem(group + side, 2)
            if len(pieces) == 2:
                src, index = pieces[side], ()
            else:
                src, index = pieces[0], (half if here and stride else side,)
            to = pl.ds(pl.multiple_of(base + half * (stride or part), part), part)
            for c in range(dst.shape[1] // cols if cols else 1):
                from_rows = slice(start + c * part, start + (c + 1) * part)
                from_cols = slice(lanes[0], lanes[0] + lanes[1]) if lanes else slice(None)
                to_cols = slice(c * cols, (c + 1) * cols) if cols else slice(None)
                source, target = index + (from_rows, from_cols), (to, to_cols)
                if sems is None:
                    moves[kind, r].append((src, source, dst, target))
                else:
                    at = pl.ds(start + c * part, part)
                    copy = pltpu.make_async_copy(
                        src.at[index + (at, slice(None))], dst.at[target], sems.at[used[0]]
                    )
                    used[0] += 1
                    copy.start()
                    moves[kind, r].append(copy)

    def ready(kind, r):
        for move in moves[kind, r]:
            if sems is None:
                src, source, dst, target = move
                dst[target] = src[source]
            else:
                move.wait()

    return fetch, ready


def weight_pairs(refs, counts):
    chunks, at = [], 0
    for pieces in counts:
        pairs = []
        for dh in range(lax.axis_size("head")):
            for ds in range(lax.axis_size("sub")):
                taken = pieces if dh else 1
                pairs.append(refs[at : at + taken])
                at += taken
        chunks.append(pairs)
    return chunks, refs[at:]


def first_frame(slab):
    count = lax.axis_size("head") * lax.axis_size("sub")
    return (lax.axis_index("seq") * count + member((0, 0), 1)) * slab


def conv_kernel_body(geo, *refs):
    count, halo, rim, taps = geo
    emb_ref, before_ref, after_ref = refs[:3]
    att_refs = refs[3 : 3 + count]
    chunks, refs = weight_pairs(refs[3 + count :], (2, 2))
    feat_ref, window_ref, emb_scr, w_out, w_conv, k_conv, w_mix, stream_scr, gate_scr, sems = refs
    win, model = emb_scr.shape
    slab = feat_ref.shape[0]
    first = first_frame(slab)
    total_frames = lax.axis_size("seq") * count * slab
    me = member((0, 0), 1)
    rows = emb_ref.shape[0]
    own = win - halo
    cols = before_ref.shape[1]
    window = []
    for c in range(model // cols):
        piece, lanes = pl.ds(rows + c * halo, halo), pl.ds(c * cols, cols)
        window += [
            (me == 0, before_ref.at[piece, :], emb_scr.at[pl.ds(0, halo), lanes]),
            (me == count - 1, after_ref.at[piece, :], emb_scr.at[pl.ds(own, halo), lanes]),
        ]
    window += [
        (me == 0, emb_ref.at[pl.ds(0, own), :], emb_scr.at[pl.ds(halo, own), :]),
        (me == count - 1, emb_ref.at[pl.ds(rows - own, own), :], emb_scr.at[pl.ds(0, own), :]),
        (
            (me > 0) & (me < count - 1),
            emb_ref.at[pl.ds(pl.multiple_of(jnp.clip(me * slab - halo, 0, rows - win), halo), win), :],
            emb_scr,
        ),
    ]

    def window_copies(act):
        for at, (here, src, dst) in enumerate(window):
            copy = pltpu.make_async_copy(src, dst, sems.at[at])
            pl.when(here)(lambda copy=copy: getattr(copy, act)())

    window_copies("start")
    fetch, ready = fetcher(chunks)
    out_half = w_out.shape[0] // count // 2
    mix_half = w_mix.shape[1] // 2
    tap_half = k_conv.shape[1] // 2
    deep = w_conv.shape[1] // 2
    step = deep // 2
    low_rows = step // (model // w_conv.shape[2])

    def fetch_low(r):
        at = out_half + mix_half + tap_half
        for c in range(step // low_rows):
            lanes = (c * w_conv.shape[2], w_conv.shape[2])
            fetch(
                ("low", c), r, 0, at, low_rows, w_conv.at[r], step + c * low_rows, deep, lanes=lanes
            )

    def ready_low(r):
        if r < lax.axis_size("sub"):
            ready("low", r)
        else:
            for c in range(step // low_rows):
                ready(("low", c), r)

    for r in range(count):
        fetch("out", r, 0, 0, out_half, w_out, r * 2 * out_half)
    for r in range(count):
        fetch("top", r, 1, 0, step, w_conv.at[r], 0, deep)
        if r < lax.axis_size("sub"):
            fetch("low", r, 1, step, step, w_conv.at[r], step, deep)
        else:
            fetch_low(r)
        fetch("taps", r, 0, out_half + mix_half, tap_half, k_conv.at[r], 0)
        fetch("mix", r, 0, out_half, mix_half, w_mix.at[r], 0)

    attended = jnp.concatenate([ref[...] for ref in att_refs], axis=1)
    window_copies("wait")
    for r in range(count):
        ready("out", r)
    frames = first - halo + lax.broadcasted_iota(jnp.int32, (win, 1), 0)
    inside = (frames >= 0) & (frames < total_frames)
    stream = jnp.where(inside, emb_scr[...].astype(F32) + dot(attended, w_out[...]), 0.0)
    stream_scr[...] = stream
    conv_normed = layer_norm(stream).astype(BF16)

    mid = slab + 2 * rim
    group_cols = w_conv.shape[2]
    lead = halo - rim - taps // 2
    conv_sum = jnp.zeros((mid, model), F32)
    for r in range(count):
        ready("top", r)
        ready_low(r)
        signal = dot(conv_normed, w_conv[r, deep:, :])
        gated = dot(conv_normed, w_conv[r, :deep, :]) * jax.nn.sigmoid(signal)
        gated = gated.astype(BF16).astype(F32)
        ready("taps", r)
        kernel = k_conv[r, :, : 2 * group_cols].astype(F32)
        kernel = kernel[:, :group_cols] + kernel[:, group_cols:]
        active = []
        for c in range(group_cols // LANES):
            lanes = slice(c * LANES, (c + 1) * LANES)
            gate_scr[c] = gated[:, lanes]
            depth = jnp.zeros((mid, LANES), F32)
            for k in range(taps):
                depth = depth + kernel[k : k + 1, lanes] * gate_scr[c, lead + k : lead + k + mid, :]
            active.append((depth * jax.nn.sigmoid(depth)).astype(BF16))
        ready("mix", r)
        part = dot(jnp.concatenate(active, axis=1), w_mix[r])
        conv_sum = conv_sum + part.astype(BF16).astype(F32)
    features = layer_norm(stream_scr[halo - rim : halo - rim + mid, :] + conv_sum).astype(BF16)
    feat_ref[...] = features[rim : rim + slab]
    window_ref[...] = features


def voc_kernel_body(geo, *refs):
    count, rim, half_voc = geo
    used_ref, window_ref, voc_kernel_ref, bias_ref, table_ref, hann_ref = refs[:6]
    chunks, refs = weight_pairs(refs[6:], (2, 1))
    wave_ref, w_vin, w_up, w_down, w_head, w_table, base_scr, wave_scr, out_scr, row_scr, sems = refs
    slab = wave_ref.shape[0] * LANES // HOP
    first = first_frame(slab)
    total_frames = lax.axis_size("seq") * count * slab
    used = used_ref[0]
    owners = [member(s, -1) for s in shifts()]
    fetch, ready = fetcher(chunks, sems)
    vin_half = w_vin.shape[0] // count // 2
    down_half = w_down.shape[0] // count // 2
    up_half = w_up.shape[0] // count // 2
    head_half = w_head.shape[0] // count // 2
    voc = w_vin.shape[1]
    rest = vin_half + down_half
    for r in range(count):
        fetch("vin", r, 0, 0, vin_half, w_vin, owners[r] * 2 * vin_half)
    for r in range(count):
        fetch(
            "up", r, 0, rest, up_half, w_up, owners[r] * 2 * up_half, cols=voc
        )
    for r in range(count):
        fetch("down", r, 0, vin_half, down_half, w_down, owners[r] * 2 * down_half)
    for r in range(count):
        fetch(
            "head",
            r,
            1,
            0,
            head_half,
            w_head,
            owners[r] * 2 * head_half,
            cols=voc,
        )
    table_copy = pltpu.make_async_copy(table_ref, w_table, sems.at[sems.shape[0] - 1])
    table_copy.start()
    features = window_ref[...]
    mid = features.shape[0]

    for r in range(count):
        ready("vin", r)
    ids = first - rim + lax.broadcasted_iota(jnp.int32, (mid, 1), 0)
    live = (ids >= 0) & (ids < used)
    base = layer_norm(jnp.where(live, dot(features, w_vin[...]), 0.0))
    voc = base.shape[1]
    trim = half_voc + 1
    rows = mid - 2 * trim
    depth = []
    for c in range(voc // LANES):
        lanes = slice(c * LANES, (c + 1) * LANES)
        base_scr[c] = base[:, lanes]
        total = jnp.zeros((rows, LANES), F32)
        for k in range(2 * half_voc + 1):
            total = total + voc_kernel_ref[k : k + 1, lanes] * base_scr[c, 1 + k : 1 + k + rows, :]
        depth.append(total)
    inner = jnp.concatenate(
        [p.astype(BF16) for p in normalize(depth, voc)], axis=1
    )
    for r in range(count):
        ready("up", r)
    up = dot(inner, w_up[...])
    hidden = (0.5 * up * (1.0 + lax.erf(up * math.sqrt(0.5)))).astype(BF16)
    for r in range(count):
        ready("down", r)
    center = jnp.concatenate(
        [base_scr[c, trim : trim + rows, :] for c in range(voc // LANES)], axis=1
    )
    head_input = layer_norm(center + dot(hidden, w_down[...])).astype(BF16)
    for r in range(count):
        ready("head", r)
    spectrum = dot(head_input, w_head[...]) + bias_ref[...]
    bins = spectrum.shape[1] // 2
    magnitude = jnp.minimum(jnp.exp(spectrum[:, :bins]), 100.0)
    sine, cosine = sine_cosine(spectrum[:, bins:])
    coefficients = jnp.concatenate([magnitude * cosine, magnitude * sine], axis=1).astype(BF16)
    table_copy.wait()
    ids = first - rim + trim + lax.broadcasted_iota(jnp.int32, (rows, 1), 0)
    exists = jnp.where((ids >= 0) & (ids < total_frames), 1.0, 0.0)
    parts = wave_scr.shape[0]
    span = wave_scr.shape[2]
    for q in range(parts):
        wave_scr[q] = exists * dot(coefficients, w_table[:, q * span : (q + 1) * span])
    audio = jnp.zeros((slab, span), F32)
    energy = jnp.zeros((slab, span), F32)
    for q in range(parts):
        begin = rim - trim + parts // 2 - q
        audio = audio + wave_scr[q, begin : begin + slab, :]
        energy = energy + exists[begin : begin + slab] * hann_ref[q : q + 1, :]
    audio = audio / energy
    tiles = range(span // LANES)
    for c in tiles:
        out_scr[c, :slab, :] = audio[:, c * LANES : (c + 1) * LANES]
    even, odd = (
        jnp.concatenate([out_scr[c, pl.ds(at, slab // 2, stride=2), :] for c in tiles], axis=1)
        for at in range(2)
    )
    samples = jnp.concatenate([even[:, :HOP], odd[:, :HOP]], axis=1)
    count = 2 * HOP // LANES
    for c in range(count):
        row_scr[pl.ds(c, slab // 2, stride=count), :] = samples[:, c * LANES : (c + 1) * LANES]
    wave_ref[...] = row_scr[: wave_ref.shape[0], :]


def synthesis(bins, padded, span):
    size = 2 * (bins - 1)
    parts = size // HOP
    k = np.arange(bins)[:, None]
    n = np.arange(size)[None, :]
    angle = 2.0 * np.pi / size * (k * n % size)
    hann = 0.5 - 0.5 * np.cos(2.0 * np.pi / size * np.arange(size))
    edge = (k == 0) | (k == bins - 1)
    factor = np.where(edge, 1.0, 2.0) / size * hann[None, :]
    both = (factor * np.cos(angle), np.where(edge, 0.0, -factor * np.sin(angle)))
    table = np.zeros((2, padded, parts, span), np.float32)
    for at, values in enumerate(both):
        table[at, :bins, :, :HOP] = values.reshape(bins, parts, HOP)
    squares = np.ones((parts, span), np.float32)
    squares[:, :HOP] = (hann * hann).reshape(parts, HOP)
    return table.reshape(2 * padded, parts * span).astype(ml_dtypes.bfloat16), squares


def local(
    tokens,
    masked,
    used_frames,
    tables,
    mask_vec,
    attn_in,
    head_temp,
    attn_out,
    conv_in,
    conv_kernel,
    conv_out,
    voc_in,
    voc_kernel,
    voc_up,
    voc_down,
    voc_head,
    head_bias,
):
    frame_count = tokens.shape[1]
    count = lax.axis_size("head") * lax.axis_size("sub")
    seq_size = lax.axis_size("seq")
    model = attn_in.shape[1]
    piece_cols = tables.shape[2]
    cols = attn_in.shape[2]
    width = round_up(cols, LANES)
    head_size = cols // head_temp.shape[0]
    slab = frame_count // count
    bins = head_bias.shape[0] // 2
    half_voc = voc_kernel.shape[0] // 2
    parts = 2 * (bins - 1) // HOP
    rim = round_up(half_voc + parts // 2, 8)
    halo = round_up(half_voc + parts // 2 + conv_kernel.shape[0] // 2, EDGE)
    win = slab + 2 * halo
    mid = slab + 2 * rim
    taps = conv_kernel.shape[0]

    others = range(1, lax.axis_size("head"))
    group = lax.rem(lax.axis_index("groups"), 2)
    deep = conv_in.shape[1]

    def cross(x):
        return [rotate(x, "head", dh) for dh in others]

    def spread(xs):
        return [rotate(x, "groups", 1) for x in xs]

    def share(xs):
        return [rotate(x, "sub", 1) for x in xs]

    near, far, near_sub, far_sub, own, own_sub, mine = {}, {}, {}, {}, {}, {}, {}
    mine["top"] = lax.dynamic_slice(
        conv_in, (group, 0, 0), (1, deep // 2, conv_in.shape[2])
    ).reshape(deep // 2, conv_in.shape[2])
    own["b"] = conv_in
    near["top"] = cross(mine["top"])
    own_sub["b"] = share([own["b"]])

    embedded = call(
        embed_kernel,
        jax.ShapeDtypeStruct((frame_count, piece_cols), BF16),
        [VMEM] * 4,
        VMEM,
        [],
        1,
        "embed",
    )(tokens, masked[None, :], tables, mask_vec)
    crossed = cross(embedded)
    beside = share([embedded])
    [conv_kernel], [embedded], near["top"] = together([conv_kernel], [embedded], near["top"])

    padded = round_up(bins, LANES)
    gap = ((0, 0), (0, padded - bins))
    bias = jnp.pad(head_bias.reshape(2, bins), gap).reshape(1, 2 * padded)
    tap_rows = round_up(taps, 32)
    voc = voc_in.shape[1]
    first_rows = (attn_out.shape[0] + conv_out.shape[0] + tap_rows) // 2
    low_rows = deep // 2 * conv_in.shape[2] // model
    conv_rows = (voc_in.shape[0] + voc_down.shape[0]) // 2
    conv_rows += voc_up.shape[0] * voc_up.shape[1] // voc // 2
    head_rows = voc_head.shape[0] * 2 * padded // voc // 2
    packed = call(
        pack_kernel,
        [
            jax.ShapeDtypeStruct((2, first_rows, model), BF16),
            jax.ShapeDtypeStruct((2, conv_rows, voc), BF16),
            jax.ShapeDtypeStruct((2, head_rows, voc), BF16),
            jax.ShapeDtypeStruct((first_rows + low_rows, model), BF16),
            jax.ShapeDtypeStruct((conv_rows, voc), BF16),
        ],
        [HBM] * 6 + [VMEM] * 2,
        [VMEM] * 5,
        [
            pltpu.VMEM((tap_rows, model), BF16),
            pltpu.VMEM((voc_head.shape[0], 2 * padded), BF16),
            pltpu.SemaphoreType.DMA((48,)),
        ],
        1,
        "pack",
    )(attn_out, conv_in, conv_out, voc_in, voc_up, voc_down, conv_kernel, voc_head.T)

    own["a"], own["c"], own["h"], mine["a"], mine["c"] = packed
    near["a"] = cross(mine["a"])

    crossed, beside, own_sub["b"], [own["a"], own["c"], own["h"], mine["c"]] = together(
        crossed, beside, own_sub["b"], [own["a"], own["c"], own["h"], mine["c"]]
    )

    def members(own_piece, beside_piece, others_pieces):
        pieces = [own_piece] + beside_piece
        for piece in others_pieces:
            pieces += [piece] + share([piece])
        return pieces

    pieces = members(embedded, beside, crossed)
    for kind in ("a", "c"):
        own_sub[kind] = share([own[kind]])
    chunk = 2 * width
    message = (frame_count + (model // chunk + 1) * halo, chunk)
    q_own, emb, upward, downward = call(
        lambda *refs: project_kernel(count, head_size, *refs),
        (
            jax.ShapeDtypeStruct((frame_count, width), BF16),
            jax.ShapeDtypeStruct((frame_count, model), BF16),
            jax.ShapeDtypeStruct(message, BF16),
            jax.ShapeDtypeStruct(message, BF16),
        ),
        [VMEM] * (count + 1),
        (VMEM,) * 4,
        [pltpu.VMEM((model, 3 * width), BF16)],
        1,
        "project",
    )(*pieces, attn_in)

    below, above = rotate(upward, "seq", 1), rotate(downward, "seq", -1)
    heads = head_temp.shape[0]

    def attend(hops, blocks, sums, cost):
        return call(
            lambda *refs: attend_part_kernel(head_size, hops, *refs),
            jax.ShapeDtypeStruct((heads, frame_count, chunk), F32),
            [SMEM, SMEM] + [VMEM] * (1 + len(blocks) + len(sums)),
            VMEM,
            [pltpu.VMEM((len(blocks), frame_count, chunk), BF16)],
            cost,
            "attend",
        )(used_frames, head_temp, q_own, *blocks, *sums)

    [q_own], near["top"], own_sub["a"], own_sub["c"] = together(
        [q_own], near["top"], own_sub["a"], own_sub["c"]
    )
    far["top"] = spread(near["top"])
    sums = attend([0], [upward], [], COSTS[0])
    [sums, mine["c"]], near["a"], far["top"] = together([sums, mine["c"]], near["a"], far["top"])
    far["a"], near["c"] = spread(near["a"]), cross(mine["c"])
    near_sub["a"] = share(near["a"])
    [below, sums] = together([below, sums])[0]
    blocks, hops = [upward, below, above], [0, -1, 1]
    ahead, behind = below[:frame_count], above[:frame_count]
    for hop in range(2, seq_size // 2 + 1):
        ahead = rotate(ahead, "seq", 1)
        blocks.append(ahead)
        hops.append(-hop)
        if 2 * hop < seq_size:
            behind = rotate(behind, "seq", -1)
            blocks.append(behind)
            hops.append(hop)
    sums = attend([-1], [below], [sums], COSTS[1])
    sums = attend([1], [above], [sums], COSTS[2])
    last, [sums], near["top"], far["top"], near_sub["a"] = together(
        blocks[3:], [sums], near["top"], far["top"], near_sub["a"]
    )
    blocks[3:] = last
    near_sub["top"], far_sub["top"] = share(near["top"]), share(far["top"])
    windows = call(
        lambda *refs: attend_last_kernel(head_size, halo, hops, 3, count, slab, *refs),
        (jax.ShapeDtypeStruct((win, cols), BF16),) * count,
        [SMEM, SMEM] + [VMEM] * (4 + len(blocks)),
        (VMEM,) * count,
        [
            pltpu.VMEM((len(blocks), frame_count, chunk), BF16),
            pltpu.VMEM((frame_count + 2 * halo, width), BF16),
        ],
        COSTS[3],
        "attend_last",
    )(used_frames, head_temp, q_own, sums, below, above, *blocks)

    windows, near_sub["top"], far_sub["top"], far["a"], near["c"] = together(
        windows, near_sub["top"], far_sub["top"], far["a"], near["c"]
    )
    attended = send_members(windows)
    far_sub["a"], far["c"] = share(far["a"]), spread(near["c"])
    attended, far_sub["a"], near["c"], [own["h"]] = together(
        attended, far_sub["a"], near["c"], [own["h"]]
    )
    near["h"], near_sub["c"] = cross(own["h"]), share(near["c"])
    own_sub["h"] = share([own["h"]])
    own["top"], own_sub["top"] = own["b"], own_sub["b"]

    def weights(kind):
        found = [own[kind], *own_sub[kind]]
        for dh in range(len(others)):
            found += [t[kind][dh] for t in (near, far, near_sub, far_sub) if kind in t]
        return found

    conv_weights = [w for kind in ("a", "top") for w in weights(kind)]
    span = round_up(HOP, LANES)
    table, squares = synthesis(bins, padded, span)
    features, window = call(
        lambda *refs: conv_kernel_body((count, halo, rim, taps), *refs),
        (
            jax.ShapeDtypeStruct((slab, model), BF16),
            jax.ShapeDtypeStruct((mid, model), BF16),
        ),
        [HBM] * 3 + [VMEM] * (count + len(conv_weights)),
        (VMEM, VMEM),
        [
            pltpu.VMEM((win, model), BF16),
            pltpu.VMEM((count * cols, model), BF16),
            pltpu.VMEM((count, 2 * deep, conv_in.shape[2]), BF16),
            pltpu.VMEM((count, tap_rows, model), BF16),
            pltpu.VMEM((count,) + conv_out.shape, BF16),
            pltpu.VMEM((win, model), F32),
            pltpu.VMEM((conv_in.shape[2] // LANES, win, LANES), F32),
            pltpu.SemaphoreType.DMA((3 + 2 * model // (2 * width),)),
        ],
        0,
        "conv",
    )(emb, below, above, *attended, *conv_weights)
    [window], far["c"], near_sub["c"], near["h"], own_sub["h"] = together(
        [window], far["c"], near_sub["c"], near["h"], own_sub["h"]
    )
    far_sub["c"], near_sub["h"] = share(far["c"]), share(near["h"])
    voc_weights = weights("c") + weights("h")
    wave = call(
        lambda *refs: voc_kernel_body((count, rim, half_voc), *refs),
        jax.ShapeDtypeStruct((slab * HOP // LANES, LANES), F32),
        [SMEM] + [VMEM] * 3 + [HBM, VMEM] + [HBM] * len(voc_weights),
        VMEM,
        [
            pltpu.VMEM((count * voc_in.shape[0], voc), BF16),
            pltpu.VMEM((count * voc_up.shape[0], voc_up.shape[1]), BF16),
            pltpu.VMEM((count * voc_down.shape[0], voc), BF16),
            pltpu.VMEM((count * voc_head.shape[0], 2 * padded), BF16),
            pltpu.VMEM(table.shape, BF16),
            pltpu.VMEM((voc // LANES, mid, LANES), F32),
            pltpu.VMEM((parts, mid - 2 * (half_voc + 1), span), F32),
            pltpu.VMEM((span // LANES, slab + 8, LANES), F32),
            pltpu.VMEM((slab * HOP // LANES + 8, LANES), F32),
            pltpu.SemaphoreType.DMA((4 * count + 4 * count * (voc_up.shape[1] // voc) + 1,)),
        ],
        1,
        "vocoder",
    )(
        used_frames,
        window,
        voc_kernel,
        bias,
        jnp.asarray(table),
        jnp.asarray(squares),
        *voc_weights,
    )
    return features, wave.reshape(slab * HOP)


def solution(mesh):
    in_specs = (
        P(None, ("groups", "seq")),
        P(("groups", "seq")),
        P("groups"),
        P(None, None, ("head", "sub")),
        P(("head", "sub")),
        P(None, None, ("head", "sub")),
        P(("head", "sub")),
        P(("head", "sub"), None),
        P(None, None, ("head", "sub")),
        P(None, ("head", "sub")),
        P(("head", "sub"), None),
        P(("head", "sub"), None),
        P(),
        P(("head", "sub"), None),
        P(("head", "sub"), None),
        P(("head", "sub"), None),
        P(),
    )
    out_specs = (P(("groups", "seq", "head", "sub"), None), P(("groups", "seq", "head", "sub")))
    return jax.shard_map(local, mesh=mesh, in_specs=in_specs, out_specs=out_specs, check_vma=False)
```
